32 devices in a mesh: grp: 2 (over y), hid: 4 (over z), ex: 2 (over x), sub: 2 (over core).
Axes of the slice: x: 2, y: 2, z: 4, core: 2. Of those that a mesh axis runs over, the one named last changes fastest.
Arguments:
- cand_grad: bfloat16 [512, 11008], P(('grp', 'ex'), 'hid'), parts along dimension 0, may hold values from -6 to 6
- query_grad: bfloat16 [512, 11008], P(('grp', 'ex'), 'hid'), parts along dimension 0, may hold values from -6 to 6
- cand_act: bfloat16 [512, 4096], P(('grp', 'ex'), 'sub'), parts along dimension 0, may hold values from -6 to 6
- query_act: bfloat16 [512, 4096], P(('grp', 'ex'), 'sub'), parts along dimension 0, may hold values from -6 to 6
- cand_ids: int32 [512], P(('grp', 'ex')), parts along dimension 0, may hold values from 1 to 50279, as said below
- query_ids: int32 [512], P(('grp', 'ex')), parts along dimension 0, may hold values from 1 to 50279, as said below
- cand_offsets: int32 [8], P('grp'), parts along dimension 0, may hold values from 0 to 255, as said below
- basis_g: bfloat16 [11008, 11008], P('hid', ('ex', 'sub')), may hold values from -0.0546875 to 0.0546875
- basis_a: bfloat16 [4096, 4096], P('sub', 'hid'), may hold values from -0.09375 to 0.09375
- eigvals: float32 [11008, 4096], P('ex', 'hid'), may hold values from 0.25 to 4
Outputs:
- scores: float32 [8, 16], P('grp', 'sub'), parts along dimension 0
The draws below stay inside these ranges and needn't reach their ends.
There are 2 independent parts, one for each index of `grp`. The reference program is written for one: setup_inputs(seed, part) draws one part's arguments, and reference() takes and returns one part's arrays. A program takes and returns all parts, laid end to end along the dimension named above; an argument that names none is the same for every part. Nothing has to cross between parts.
Inputs may be any that keep to these rules, and one draw needn't show every extreme that they name: `cand_ids`: token id 1 is padding; all other ids are real tokens. `query_ids`: token id 1 is padding; all other ids are real tokens. cand_offsets[0] is 0 and the offsets rise strictly, so every example holds one or more tokens.
All inputs are finite; a program needn't handle non-finite values.
Results may differ from the reference program's by a relative error of at most 0.0056.
Values may be sent and summed in bfloat16 or wider, within the bound.
No kernel may reach another device: no remote copies, remote signals or barrier semaphores. Data moves between devices by JAX's collectives and lax.ppermute only.
A program may use at most 192 MiB of HBM per device.

```python
import math
import jax
import jax.numpy as jnp
from jax import lax

D = 4096
FF = 11008
VOCAB = 50280
TC_DEV = 128
EX_DEV = 2
QLEN = 16
TC = 256
NEXC = 4
NQ = 16
TQ = 256


def token_draw(key, count):
    first_key, second_key = jax.random.split(key)
    real_ids = jax.random.randint(first_key, (count,), 2, VOCAB)
    padding = jax.random.randint(second_key, (count,), 0, 4)
    token_ids = jnp.where(padding == 0, 1, real_ids).astype(jnp.int32)
    token_ids = token_ids.at[count // 2].set(1)
    token_ids = token_ids.at[count - 1].set(VOCAB - 1)
    return token_ids.astype(jnp.int32)


def draw_cand_ids(key, part):
    key = jax.random.fold_in(key, 11)
    return token_draw(key, TC)


def draw_query_ids(key, part):
    key = jax.random.fold_in(key, 17)
    return token_draw(key, TQ)


def draw_cand_offsets(key, part):
    key = jax.random.fold_in(key, 23)
    inner = jax.random.permutation(key, TC - 1)[:NEXC - 1] + 1
    return jnp.concatenate([jnp.zeros((1,), jnp.int32), jnp.sort(inner).astype(jnp.int32)])


def block_scale(stream_key, extent, pieces, least, largest):
    loudness = 1.0
    for position, shards_of in pieces:
        draws = jax.random.uniform(jax.random.fold_in(jax.random.fold_in(stream_key, 6), position), (shards_of,), jnp.float32, least / len(pieces), largest / len(pieces))
        loudness = loudness * jnp.repeat(jnp.exp(draws), extent[position] // shards_of).reshape((-1,) + (1,) * (len(extent) - 1 - position))
    return loudness


def centred(stream_key, dims, deviation, bound, cuts=(), kind=jnp.bfloat16):
    values = jax.random.normal(stream_key, dims, jnp.float32) * deviation
    if len(cuts) > 0:
        values = block_scale(stream_key, dims, cuts, -0.22, 0.18) * values
    return jnp.clip(values, min=-bound, max=bound).astype(kind)


def setup_inputs(seed: int = 0, part: int = 0) -> dict:
    key_list = jax.random.split(jax.random.key(seed), 11)
    own_keys = jax.random.split(jax.random.fold_in(key_list[10], part), 11)
    cand_grad = centred(own_keys[0], (TC, FF), 1.0, 6.0, ((0, 2), (1, 4)))
    query_grad = centred(own_keys[1], (TQ, FF), 1.0, 6.0, ((0, 2), (1, 4)))
    cand_act = centred(own_keys[2], (TC, D), 1.0, 6.0, ((0, 2), (1, 2)))
    query_act = centred(own_keys[3], (TQ, D), 1.0, 6.0, ((0, 2), (1, 2)))
    cand_ids = draw_cand_ids(jax.random.fold_in(jax.random.fold_in(key_list[10], part), 71), part)
    query_ids = draw_query_ids(jax.random.fold_in(jax.random.fold_in(key_list[10], part), 71), part)
    cand_offsets = draw_cand_offsets(jax.random.fold_in(jax.random.fold_in(key_list[10], part), 71), part)
    basis_g = centred(key_list[7], (FF, FF), FF ** -0.5, 0.0546875, ((0, 4), (1, 4)))
    basis_a = centred(key_list[8], (D, D), D ** -0.5, 0.09375, ((0, 2), (1, 4)))
    eigvals = jnp.clip(jnp.exp(math.log(4.0) - 2.7725887 * jax.random.uniform(key_list[9], (FF, D), jnp.float32) ** block_scale(key_list[9], (FF, D), ((0, 2), (1, 4)), -0.2, 0.2)), 0.25, 4.0)
    return {"cand_grad": cand_grad, "query_grad": query_grad, "cand_act": cand_act, "query_act": query_act, "cand_ids": cand_ids, "query_ids": query_ids, "cand_offsets": cand_offsets, "basis_g": basis_g, "basis_a": basis_a, "eigvals": eigvals}


pad_token = 1

def project_grads(grad_rows, token_ids, basis_g):
    keep_rows = (token_ids != pad_token).astype(jnp.bfloat16)[:, None]
    return jnp.dot(grad_rows * keep_rows, basis_g, preferred_element_type=jnp.float32).astype(jnp.bfloat16)

def reference(cand_grad, query_grad, cand_act, query_act, cand_ids, query_ids, cand_offsets, basis_g, basis_a, eigvals):
    eig_cand_grad = project_grads(cand_grad, cand_ids, basis_g)
    eig_query_grad = project_grads(query_grad, query_ids, basis_g)
    eig_cand_act = jnp.dot(cand_act, basis_a, preferred_element_type=jnp.float32).astype(jnp.bfloat16)
    eig_query_act = jnp.dot(query_act, basis_a, preferred_element_type=jnp.float32).astype(jnp.bfloat16)
    query_grads = eig_query_grad.reshape(NQ, QLEN, FF)
    query_acts = eig_query_act.reshape(NQ, QLEN, D)
    cand_wide = eig_cand_act.astype(jnp.float32)

    def one_query(query_pair):
        grad_block, act_block = query_pair
        outer_sum = jnp.dot(grad_block.T, act_block, preferred_element_type=jnp.float32)
        precond = (outer_sum / eigvals).astype(jnp.bfloat16)
        image_rows = jnp.dot(eig_cand_grad, precond, preferred_element_type=jnp.float32)
        return lax.optimization_barrier(jnp.sum(image_rows * cand_wide, axis=1))
    token_scores = lax.map(one_query, (query_grads, query_acts))
    positions = jnp.arange(TC, dtype=jnp.int32)
    example_ends = jnp.concatenate([cand_offsets[1:], jnp.full((1,), TC, jnp.int32)])
    member = ((positions[None, :] >= cand_offsets[:, None]) & (positions[None, :] < example_ends[:, None])).astype(jnp.float32)
    factor = 1.0 / math.sqrt(FF * D * QLEN * (TC_DEV // EX_DEV))
    return jnp.dot(member, token_scores.T, precision=lax.Precision.HIGHEST) * factor
```

```python
import functools
import math

import jax
import jax.numpy as jnp
from jax import lax
from jax.experimental import pallas as pl
from jax.experimental.pallas import tpu as pltpu
from jax.sharding import PartitionSpec as P

D = 4096
FF = 11008
TC_DEV = 128
EX_DEV = 2
QLEN = 16
PAD = 1
VMEM_BYTES = 48 * 1024 * 1024
CHUNKS = (256, 640, 640, 640, 384)


def chunk_bounds(total):
    bounds = []
    start = 0
    for width in CHUNKS:
        if start + width < total:
            bounds.append((start, width))
            start += width
    bounds.append((start, total - start))
    return bounds


def project_kernel(n_first, n_second, *refs):
    firsts = refs[:n_first]
    seconds = refs[n_first : n_first + n_second]
    basis_ref, out_ref, rows_ref = refs[n_first + n_second :]
    split = firsts[0].shape[0]

    @pl.when(pl.program_id(0) == 0)
    def _():
        rows_ref[:split] = functools.reduce(lambda a, b: a + b, [r[...] for r in firsts])
        rows_ref[split:] = functools.reduce(lambda a, b: a + b, [r[...] for r in seconds])

    out_ref[...] = jnp.dot(
        rows_ref[...], basis_ref[...], preferred_element_type=jnp.float32
    ).astype(out_ref.dtype)


def project(firsts, seconds, basis, start, width, out_type):
    rows = firsts[0].shape[0] + seconds[0].shape[0]
    depth = basis.shape[0]
    tile = 256 if width % 256 == 0 and start % 256 == 0 else 128
    tiles = pl.cdiv(width, tile)
    first_tile = start // tile
    whole = lambda a: pl.BlockSpec(a.shape, lambda i: (0, 0))
    return pl.pallas_call(
        functools.partial(project_kernel, len(firsts), len(seconds)),
        grid=(tiles,),
        in_specs=[whole(a) for a in firsts]
        + [whole(a) for a in seconds]
        + [pl.BlockSpec((depth, tile), lambda i: (0, first_tile + i))],
        out_specs=pl.BlockSpec((rows, tile), lambda i: (0, i)),
        out_shape=jax.ShapeDtypeStruct((rows, width), out_type),
        scratch_shapes=[pltpu.VMEM((rows, depth), basis.dtype)],
        compiler_params=pltpu.CompilerParams(vmem_limit_bytes=VMEM_BYTES),
        cost_estimate=pl.CostEstimate(
            flops=2 * rows * depth * width,
            bytes_accessed=2 * (rows * depth + depth * width + rows * width),
            transcendentals=0,
        ),
        name="project",
    )(*firsts, *seconds, basis)


def score_kernel(blocks, cand_rows, examples, at_ref, *refs):
    del at_ref
    sums = []
    place = 0
    for terms in blocks:
        parts = [r[...].astype(jnp.float32) for r in refs[place : place + terms]]
        sums.append(functools.reduce(lambda a, b: a + b, parts))
        place += terms
    eig_ref, cand_act_ref, query_act_ref, out_ref = refs[place:]
    cand = jnp.concatenate([b[:cand_rows] for b in sums], 0).T.astype(jnp.bfloat16)
    query = (
        jnp.concatenate([b[cand_rows:] for b in sums], 0)
        .astype(jnp.bfloat16)
        .astype(jnp.float32)
        .T
    )
    inverse = 1.0 / eig_ref[...]
    features = inverse.shape[1]
    for k in range(examples):
        outer = jnp.dot(
            cand,
            cand_act_ref[:, k * features : (k + 1) * features],
            preferred_element_type=jnp.float32,
        )
        weights = (outer * inverse).astype(jnp.bfloat16)
        image = lax.dot_general(
            weights,
            query_act_ref[...],
            (((1,), (1,)), ((), ())),
            preferred_element_type=jnp.float32,
        )
        out_ref[k : k + 1, :] = jnp.sum(image * query, axis=0, keepdims=True)


def score_chunk(blocks, cand_rows, eigvals, first_row, width, cand_acts, query_acts, examples):
    flat = [a for block in blocks for a in block]
    tokens = query_acts.shape[0]
    features = eigvals.shape[1]
    whole = lambda a: pl.BlockSpec(a.shape, lambda i, at: (0, 0))
    return pl.pallas_call(
        functools.partial(score_kernel, tuple(len(b) for b in blocks), cand_rows, examples),
        grid_spec=pltpu.PrefetchScalarGridSpec(
            num_scalar_prefetch=1,
            grid=(1,),
            in_specs=[whole(a) for a in flat]
            + [
                pl.BlockSpec(
                    (pl.Element(width), pl.Element(features)), lambda i, at: (pl.multiple_of(at[0], 8), 0)
                ),
                whole(cand_acts),
                whole(query_acts),
            ],
            out_specs=pl.BlockSpec((examples, tokens), lambda i, at: (0, 0)),
        ),
        out_shape=jax.ShapeDtypeStruct((examples, tokens), jnp.float32),
        compiler_params=pltpu.CompilerParams(vmem_limit_bytes=VMEM_BYTES),
        cost_estimate=pl.CostEstimate(
            flops=4 * width * features * tokens * examples,
            bytes_accessed=4 * width * features + 2 * cand_acts.size + 2 * query_acts.size,
            transcendentals=0,
        ),
        name="score",
    )(jnp.reshape(first_row, (1,)).astype(jnp.int32), *flat, eigvals, cand_acts, query_acts)


def line_sum_terms(own, axis, link_type):
    size = lax.axis_size(axis)
    terms = [own]
    last = None
    for hop in range(1, size):
        send = own if last is None else own.astype(jnp.float32) + last.astype(jnp.float32)
        pairs = [(hop - 1, hop), (size - hop, size - hop - 1)]
        last = lax.ppermute(send.astype(link_type), axis, pairs)
        terms.append(last)
    return terms


def small_sum(value, axes):
    size = lax.axis_size(axes)
    if size > 4:
        return lax.psum(value, axes)
    terms = [value]
    for other in range(1, size):
        terms.append(lax.ppermute(value, axes, [(i, i ^ other) for i in range(size)]))
    while len(terms) > 1:
        terms = [a + b for a, b in zip(terms[::2], terms[1::2])]
    return terms[0]


def per_device(
    cand_grad,
    query_grad,
    cand_act,
    query_act,
    cand_ids,
    query_ids,
    cand_offsets,
    basis_g,
    basis_a,
    eigvals,
):
    cand_rows = cand_grad.shape[0]
    query_rows = query_grad.shape[0]
    groups = lax.axis_size("ex")
    halves = lax.axis_size("sub")
    ex = lax.axis_index("ex")
    sub = lax.axis_index("sub")
    directions = basis_g.shape[1]
    features = basis_a.shape[1]
    examples = cand_offsets.shape[0]
    link_type = jnp.bfloat16 if lax.axis_size("hid") <= 4 else jnp.float32
    paired = groups == 2 and halves == 2 and cand_rows == query_rows
    both = ("ex", "sub")

    if paired:
        cand_over = lax.ppermute(cand_grad, both, [(0, 2), (2, 0)])
        query_over = lax.ppermute(query_grad, both, [(1, 3), (3, 1)])
        cand_across = lax.ppermute(cand_over, both, [(0, 1), (2, 3)])
        query_across = lax.ppermute(query_over, both, [(1, 0), (3, 2)])
        sources = [
            ([cand_grad], [query_grad]),
            ([cand_over, cand_across], [query_over, query_across]),
        ]
        block_cand = cand_rows
    else:
        gather = lambda a: lax.all_gather(a, "ex", axis=0, tiled=True)
        sources = [([gather(cand_grad)], [gather(query_grad)])]
        block_cand = cand_rows * groups

    bounds = chunk_bounds(directions)
    block_terms = []
    for firsts, seconds in sources:
        block_terms.append(
            [
                line_sum_terms(
                    project(firsts, seconds, basis_g, start, width, link_type), "hid", link_type
                )
                for start, width in bounds
            ]
        )

    keep = (jnp.concatenate([cand_ids, query_ids]) != PAD).astype(jnp.bfloat16)
    act_share = project([cand_act], [query_act], basis_a, 0, features, jnp.float32)
    if paired:
        to_other = jnp.where(sub == 0, act_share[cand_rows:], act_share[:cand_rows])
        mine = jnp.where(sub == 0, act_share[:cand_rows], act_share[cand_rows:])
        keep_mine = jnp.where(sub == 0, keep[:cand_rows], keep[cand_rows:])
        came = lax.ppermute(to_other, "sub", [(0, 1), (1, 0)])
        half_own = (mine + came).astype(jnp.bfloat16) * keep_mine[:, None]
        half_over = lax.ppermute(half_own, "ex", [(0, 1), (1, 0)])
        kept = jnp.concatenate([half_own, half_over], 0)
        swapped = lax.ppermute(kept, "sub", [(0, 1), (1, 0)])
        cand_eigen_act = jnp.where(sub == 0, kept, swapped)
        query_eigen_act = jnp.where(sub == 0, swapped, kept)
        span = jnp.arange(cand_rows, dtype=jnp.int32)
        positions = jnp.concatenate([ex * cand_rows + span, (1 - ex) * cand_rows + span])
    else:
        eigen = lax.psum(act_share, "sub").astype(jnp.bfloat16) * keep[:, None]
        cand_eigen_act = lax.all_gather(eigen[:cand_rows], "ex", axis=0, tiled=True)
        query_eigen_act = lax.all_gather(eigen[cand_rows:], "ex", axis=0, tiled=True)
        positions = jnp.arange(groups * cand_rows, dtype=jnp.int32)

    total_cand = groups * cand_rows
    example_ends = jnp.concatenate([cand_offsets[1:], jnp.full((1,), total_cand, jnp.int32)])
    member = (positions[:, None] >= cand_offsets[None, :]) & (
        positions[:, None] < example_ends[None, :]
    )
    split_acts = (
        member.astype(jnp.bfloat16)[:, :, None] * cand_eigen_act[:, None, :]
    ).reshape(total_cand, examples * features)

    token_scores = 0.0
    for c, (start, width) in enumerate(bounds):
        token_scores += score_chunk(
            [terms[c] for terms in block_terms],
            block_cand,
            eigvals,
            sub * directions + start,
            width,
            split_acts,
            query_eigen_act,
            examples,
        )
    queries = groups * query_rows // QLEN
    partial_value = token_scores.reshape(examples, queries, QLEN).sum(2)
    if paired:
        turned = jnp.roll(partial_value, queries // 2, axis=1)
        partial_value = jnp.where(ex == 0, partial_value, turned)
    total = small_sum(small_sum(partial_value, both), "hid")
    mine = lax.dynamic_slice_in_dim(total, sub * (queries // halves), queries // halves, 1)
    factor = 1.0 / math.sqrt(FF * D * QLEN * (TC_DEV // EX_DEV))
    return mine * factor


def solution(mesh):
    return jax.shard_map(
        per_device,
        mesh=mesh,
        in_specs=(
            P(("grp", "ex"), "hid"),
            P(("grp", "ex"), "hid"),
            P(("grp", "ex"), "sub"),
            P(("grp", "ex"), "sub"),
            P(("grp", "ex")),
            P(("grp", "ex")),
            P("grp"),
            P("hid", ("ex", "sub")),
            P("sub", "hid"),
            P("ex", "hid"),
        ),
        out_specs=P("grp", "sub"),
        check_vma=False,
    )
```

```python
import functools
import math

import jax
import jax.numpy as jnp
from jax import lax
from jax.experimental import pallas as pl
from jax.experimental.pallas import tpu as pltpu
from jax.sharding import PartitionSpec as P

D = 4096
FF = 11008
TC_DEV = 128
EX_DEV = 2
QLEN = 16
PAD = 1
MIB = 1024 * 1024
TILE = 256
WIDTHS = (1024, 1024)
F32 = jnp.float32
BF16 = jnp.bfloat16
VMEM = pl.BlockSpec(memory_space=pltpu.VMEM)
SMEM = pl.BlockSpec(memory_space=pltpu.SMEM)
ANY = pl.BlockSpec(memory_space=pl.ANY)
HBM = pl.BlockSpec(memory_space=pltpu.HBM)
ORDER = jax.ShapeDtypeStruct((8, 128), F32)
QUICK = pl.CostEstimate(flops=1024, bytes_accessed=1024, transcendentals=0)


def params(mib):
    return pltpu.CompilerParams(vmem_limit_bytes=mib * MIB)


def chunk_bounds(total):
    bounds = []
    start = 0
    for width in WIDTHS:
        if start + width < total:
            bounds.append((start, width))
            start += width
    bounds.append((start, total - start))
    return bounds


def total_of(values):
    return functools.reduce(lambda a, b: a + b, values)


def project_kernel(terms, order_ref, *refs):
    del order_ref
    if terms:
        firsts, seconds = refs[:terms], refs[terms : 2 * terms]
        basis_ref, wide_ref, send_ref, rows_ref, done_ref = refs[2 * terms :]

        @pl.when(pl.program_id(0) == 0)
        def _():
            split = firsts[0].shape[1]
            rows_ref[:split] = total_of([r[...] for r in firsts]).T
            rows_ref[split:] = total_of([r[...] for r in seconds]).T
    else:
        rows_ref, basis_ref, wide_ref, send_ref, done_ref = refs
    product = jnp.dot(rows_ref[...], basis_ref[...], preferred_element_type=F32)
    wide_ref[...] = product
    send_ref[...] = product.astype(send_ref.dtype)
    done_ref[...] = jnp.zeros_like(done_ref)


def project(order, inputs, basis, start, width):
    depth = basis.shape[0]
    whole = lambda shape: pl.BlockSpec(shape, lambda i: (0, 0))
    if isinstance(inputs, tuple):
        firsts, seconds = inputs
        terms = len(firsts)
        arrays = list(firsts) + list(seconds)
        rows = firsts[0].shape[1] + seconds[0].shape[1]
    else:
        terms = 0
        arrays = [inputs]
        rows = inputs.shape[0]
    tiles = pl.cdiv(width, TILE)
    first_tile = start // TILE
    out_specs = [pl.BlockSpec((rows, TILE), lambda i: (0, i))] * 2
    out_shape = [
        jax.ShapeDtypeStruct((rows, width), F32),
        jax.ShapeDtypeStruct((rows, width), BF16),
    ]
    if terms:
        out_specs.append(whole((rows, depth)))
        out_shape.append(jax.ShapeDtypeStruct((rows, depth), BF16))
    out = pl.pallas_call(
        functools.partial(project_kernel, terms),
        grid=(tiles,),
        in_specs=[ANY]
        + [whole(a.shape) for a in arrays]
        + [pl.BlockSpec((depth, TILE), lambda i: (0, first_tile + i))],
        out_specs=out_specs + [whole((8, 128))],
        out_shape=out_shape + [ORDER],
        compiler_params=params(50),
        cost_estimate=QUICK,
        name="project",
    )(order, *arrays, basis)
    if terms:
        return out
    return out[0], out[1], inputs, out[2]


def act_kernel(order_ref, cand_ref, query_ref, basis_ref, away_ref, mine_ref, done_ref):
    del order_ref
    cand_first = lax.axis_index("sub") != 0

    def both(first_ref, second_ref):
        away_ref[...] = jnp.dot(first_ref[...], basis_ref[...], preferred_element_type=F32)
        mine_ref[...] = jnp.dot(second_ref[...], basis_ref[...], preferred_element_type=F32)

    @pl.when(cand_first)
    def _():
        both(cand_ref, query_ref)

    @pl.when(jnp.logical_not(cand_first))
    def _():
        both(query_ref, cand_ref)

    done_ref[...] = jnp.zeros_like(done_ref)


def act_shares(order, cand_act, query_act, basis):
    rows, depth = cand_act.shape
    features = basis.shape[1]
    tile = min(TILE, features)
    whole = lambda shape: pl.BlockSpec(shape, lambda i: (0, 0))
    return pl.pallas_call(
        act_kernel,
        grid=(features // tile,),
        in_specs=[
            ANY,
            whole((rows, depth)),
            whole((rows, depth)),
            pl.BlockSpec((depth, tile), lambda i: (0, i)),
        ],
        out_specs=[pl.BlockSpec((rows, tile), lambda i: (0, i))] * 2 + [whole((8, 128))],
        out_shape=[jax.ShapeDtypeStruct((rows, features), F32)] * 2 + [ORDER],
        compiler_params=params(16),
        cost_estimate=QUICK,
        name="acts",
    )(order, cand_act, query_act, basis)


def add_kernel(order_ref, *refs):
    del order_ref
    sum_ref, done_ref = refs[-2:]
    sum_ref[...] = total_of([r[...].astype(F32) for r in refs[:-2]]).astype(sum_ref.dtype)
    done_ref[...] = jnp.zeros_like(done_ref)


def add(order, *arrays):
    return pl.pallas_call(
        add_kernel,
        in_specs=[ANY] + [VMEM] * len(arrays),
        out_specs=[VMEM, VMEM],
        out_shape=[jax.ShapeDtypeStruct(arrays[0].shape, BF16), ORDER],
        compiler_params=params(16),
        cost_estimate=QUICK,
        name="add",
    )(order, *arrays)


def half_kernel(order_ref, mine_ref, came_ref, cand_ids_ref, query_ids_ref, half_ref, done_ref):
    del order_ref
    rows = mine_ref.shape[0]
    ids = jnp.where(lax.axis_index("sub") == 0, cand_ids_ref[...], query_ids_ref[...])
    keep = jnp.where(ids != PAD, 1.0, 0.0).astype(F32)
    keep = jnp.broadcast_to(keep, (rows, rows)).T[:, :1]
    half_ref[...] = ((mine_ref[...] + came_ref[...]) * keep).astype(BF16)
    done_ref[...] = jnp.zeros_like(done_ref)


def half_acts(order, mine, came, cand_ids, query_ids):
    return pl.pallas_call(
        half_kernel,
        in_specs=[ANY] + [VMEM] * 4,
        out_specs=[VMEM, VMEM],
        out_shape=[jax.ShapeDtypeStruct(mine.shape, BF16), ORDER],
        compiler_params=params(16),
        cost_estimate=QUICK,
        name="half_acts",
    )(order, mine, came, cand_ids[None, :], query_ids[None, :])


def split_kernel(examples, order_ref, offsets_ref, own, over, own_sw, over_sw, split_ref, query_ref, done_ref):
    del order_ref
    rows, features = own.shape
    cand_here = lax.axis_index("sub") == 0
    ex = lax.axis_index("ex")
    spot = lax.broadcasted_iota(jnp.int32, (rows, 1), 0)
    for place, kept, swapped in ((0, own, own_sw), (1, over, over_sw)):
        span = pl.ds(place * rows, rows)
        first = (ex if place == 0 else 1 - ex) * rows
        cand = jnp.where(cand_here, kept[...], swapped[...])
        query_ref[span, :] = jnp.where(cand_here, swapped[...], kept[...])
        for k in range(examples):
            member = spot + first >= offsets_ref[k]
            if k + 1 < examples:
                member = member & (spot + first < offsets_ref[k + 1])
            member = jnp.where(member, 1.0, 0.0).astype(BF16)
            split_ref[span, k * features : (k + 1) * features] = cand * member
    done_ref[...] = jnp.zeros_like(done_ref)


def split_acts(order, offsets, own, over, own_sw, over_sw):
    rows, features = own.shape
    examples = offsets.shape[0]
    return pl.pallas_call(
        functools.partial(split_kernel, examples),
        in_specs=[ANY, SMEM] + [VMEM] * 4,
        out_specs=[VMEM] * 3,
        out_shape=[
            jax.ShapeDtypeStruct((2 * rows, examples * features), BF16),
            jax.ShapeDtypeStruct((2 * rows, features), BF16),
            ORDER,
        ],
        compiler_params=params(16),
        cost_estimate=QUICK,
        name="split_acts",
    )(order, offsets, own, over, own_sw, over_sw)


def row_tiles(width):
    tiles = []
    start = 0
    while start < width:
        size = min(512, width - start)
        tiles.append((start, size))
        start += size
    return tiles


def score_kernel(blocks, pick, cand_rows, examples, first, order_ref, *refs):
    del order_ref
    per_block = 2 if pick else 1
    parts = refs[: blocks * per_block]
    eig_hbm, split_ref, query_act_ref, out_ref, done_ref, eig_ref, sems = refs[blocks * per_block :]
    width = parts[0].shape[1]
    base = lax.axis_index("sub") * (eig_hbm.shape[0] // lax.axis_size("sub")) + first
    copies = []
    for n, (start, size) in enumerate(row_tiles(width)):
        copies.append(
            pltpu.make_async_copy(
                eig_hbm.at[pl.ds(pl.multiple_of(base + start, 8), size), :],
                eig_ref.at[pl.ds(start, size), :],
                sems.at[n],
            )
        )
    for copy in copies:
        copy.start()
    sums = []
    for b in range(blocks):
        here = parts[b * per_block]
        if pick:
            spot = lax.axis_index("hid")
            inner = (spot != 0) & (spot != lax.axis_size("hid") - 1)
            sums.append(jnp.where(inner, here[...], parts[b * per_block + 1][...]))
        else:
            sums.append(here[...])
    features = eig_ref.shape[1]
    cand = jnp.concatenate([s[:cand_rows] for s in sums], 0)
    query = jnp.concatenate([s[cand_rows:] for s in sums], 0)
    scores = [0.0] * examples
    for copy, (start, size) in zip(copies, row_tiles(width)):
        copy.wait()
        cand_tile = cand[:, start : start + size].T
        query_tile = query[:, start : start + size].T.astype(F32)
        inverse = 1.0 / eig_ref[start : start + size, :]
        for k in range(examples):
            outer = jnp.dot(
                cand_tile,
                split_ref[:, k * features : (k + 1) * features],
                preferred_element_type=F32,
            )
            weights = (outer * inverse).astype(BF16)
            image = lax.dot_general(
                weights,
                query_act_ref[...],
                (((1,), (1,)), ((), ())),
                preferred_element_type=F32,
            )
            scores[k] = scores[k] + jnp.sum(image * query_tile, axis=0, keepdims=True)
    for k in range(examples):
        out_ref[k : k + 1, :] = scores[k]
    done_ref[...] = jnp.zeros_like(done_ref)


def score_chunk(order, blocks, pick, cand_rows, eigvals, first, split, query_acts, examples):
    parts = [a for block in blocks for a in block]
    width = parts[0].shape[1]
    features = eigvals.shape[1]
    return pl.pallas_call(
        functools.partial(score_kernel, len(blocks), pick, cand_rows, examples, first),
        in_specs=[ANY] + [VMEM] * len(parts) + [HBM, VMEM, VMEM],
        out_specs=[VMEM, VMEM],
        out_shape=[jax.ShapeDtypeStruct((examples, query_acts.shape[0]), F32), ORDER],
        scratch_shapes=[
            pltpu.VMEM((width, features), F32),
            pltpu.SemaphoreType.DMA((len(row_tiles(width)),)),
        ],
        compiler_params=params(44),
        cost_estimate=QUICK,
        name="score",
    )(order, *parts, eigvals, split, query_acts)


def small_sum(value, axes):
    size = lax.axis_size(axes)
    if size > 4:
        return lax.psum(value, axes)
    terms = [value]
    for other in range(1, size):
        terms.append(lax.ppermute(value, axes, [(i, i ^ other) for i in range(size)]))
    while len(terms) > 1:
        terms = [a + b for a, b in zip(terms[::2], terms[1::2])]
    return terms[0]


def token_scores_paired(
    cand_grad, query_grad, cand_act, query_act, cand_ids, query_ids, cand_offsets, basis_g, basis_a, eigvals
):
    rows = cand_grad.shape[0]
    examples = cand_offsets.shape[0]
    both = ("ex", "sub")
    bounds = chunk_bounds(basis_g.shape[1])
    count = len(bounds)
    swap = lambda a, axis: lax.ppermute(a, axis, [(0, 1), (1, 0)])
    inward = lambda a: lax.ppermute(a, "hid", [(0, 1), (3, 2)])
    across = lambda a: lax.ppermute(a, "hid", [(1, 2), (2, 1)])
    outward = lambda a: lax.ppermute(a, "hid", [(1, 0), (2, 3)])

    cand_over = lax.ppermute(cand_grad, both, [(0, 2), (2, 0)])
    query_over = lax.ppermute(query_grad, both, [(1, 3), (3, 1)])
    cand_across = lax.ppermute(cand_over, both, [(0, 1), (2, 3)])
    query_across = lax.ppermute(query_over, both, [(1, 0), (3, 2)])
    tokens = [
        ([cand_grad.T], [query_grad.T]),
        ([cand_over.T, cand_across.T], [query_over.T, query_across.T]),
    ]
    order = jnp.zeros((8, 128), F32)
    wide, came_in, came_across, summed, came_out = {}, {}, {}, {}, {}
    scores = []

    def step_project(c):
        nonlocal order
        block, q = divmod(c, count)
        wide[c], send, tokens[block], order = project(order, tokens[block], basis_g, *bounds[q])
        came_in[c] = inward(send)

    def step_across(c):
        nonlocal order
        send, order = add(order, wide[c], came_in[c])
        came_across[c] = across(send)

    def step_outward(c):
        nonlocal order
        summed[c], order = add(order, wide[c], came_in[c], came_across[c])
        came_out[c] = outward(summed[c])

    def step_score(q):
        nonlocal order
        out, order = score_chunk(
            order,
            [(summed[c], came_out[c]) for c in (q, count + q)],
            True,
            rows,
            eigvals,
            bounds[q][0],
            split,
            query_acts,
            examples,
        )
        scores.append(out)

    step_project(0)
    step_project(1)
    away, mine, order = act_shares(order, cand_act, query_act, basis_a)
    came = swap(away, "sub")
    step_across(0)
    step_project(2)
    half_own, order = half_acts(order, mine, came, cand_ids, query_ids)
    half_over = swap(half_own, "ex")
    own_swapped = swap(half_own, "sub")
    step_outward(0)
    step_across(1)
    step_project(3)
    step_across(2)
    step_outward(1)
    over_swapped = swap(half_over, "sub")
    step_project(4)
    step_across(3)
    step_outward(2)
    split, query_acts, order = split_acts(
        order, cand_offsets, half_own, half_over, own_swapped, over_swapped
    )
    step_project(5)
    step_across(4)
    step_outward(3)
    step_across(5)
    step_outward(4)
    step_score(0)
    step_outward(5)
    step_score(1)
    step_score(2)
    return total_of(scores)


def token_scores_gathered(
    cand_grad, query_grad, cand_act, query_act, cand_ids, query_ids, cand_offsets, basis_g, basis_a, eigvals
):
    gather = lambda a: lax.all_gather(a, "ex", axis=0, tiled=True)
    examples = cand_offsets.shape[0]
    features = basis_a.shape[1]
    order = jnp.zeros((8, 128), F32)
    keep = lambda ids: (ids != PAD).astype(BF16)[:, None]
    share = lambda a: lax.psum(jnp.dot(a, basis_a, preferred_element_type=F32), "sub")
    cands = gather(share(cand_act).astype(BF16) * keep(cand_ids))
    query_acts = gather(share(query_act).astype(BF16) * keep(query_ids))
    cand_rows = cands.shape[0]
    positions = jnp.arange(cand_rows, dtype=jnp.int32)
    example_ends = jnp.concatenate([cand_offsets[1:], jnp.full((1,), cand_rows, jnp.int32)])
    member = (positions[:, None] >= cand_offsets[None, :]) & (
        positions[:, None] < example_ends[None, :]
    )
    split = (member.astype(BF16)[:, :, None] * cands[:, None, :]).reshape(
        cand_rows, examples * features
    )
    tokens = ([gather(cand_grad).T], [gather(query_grad).T])
    scores = []
    for start, width in chunk_bounds(basis_g.shape[1]):
        wide, _, tokens, order = project(order, tokens, basis_g, start, width)
        total = lax.psum(wide, "hid").astype(BF16)
        out, order = score_chunk(
            order, [(total,)], False, cand_rows, eigvals, start, split, query_acts, examples
        )
        scores.append(out)
    return total_of(scores)


def per_device(
    cand_grad,
    query_grad,
    cand_act,
    query_act,
    cand_ids,
    query_ids,
    cand_offsets,
    basis_g,
    basis_a,
    eigvals,
):
    groups = lax.axis_size("ex")
    halves = lax.axis_size("sub")
    ex = lax.axis_index("ex")
    sub = lax.axis_index("sub")
    examples = cand_offsets.shape[0]
    paired = (
        groups == 2
        and halves == 2
        and lax.axis_size("hid") == 4
        and cand_grad.shape[0] == query_grad.shape[0]
    )
    arrays = (
        cand_grad, query_grad, cand_act, query_act, cand_ids, query_ids, cand_offsets, basis_g, basis_a, eigvals
    )
    token_scores = token_scores_paired(*arrays) if paired else token_scores_gathered(*arrays)
    queries = groups * query_grad.shape[0] // QLEN
    partial_value = token_scores.reshape(examples, queries, QLEN).sum(2)
    if paired:
        turned = jnp.roll(partial_value, queries // 2, axis=1)
        partial_value = jnp.where(ex == 0, partial_value, turned)
    total = small_sum(small_sum(partial_value, ("ex", "sub")), "hid")
    mine = lax.dynamic_slice_in_dim(total, sub * (queries // halves), queries // halves, 1)
    factor = 1.0 / math.sqrt(FF * D * QLEN * (TC_DEV // EX_DEV))
    return mine * factor


def solution(mesh):
    return jax.shard_map(
        per_device,
        mesh=mesh,
        in_specs=(
            P(("grp", "ex"), "hid"),
            P(("grp", "ex"), "hid"),
            P(("grp", "ex"), "sub"),
            P(("grp", "ex"), "sub"),
            P(("grp", "ex")),
            P(("grp", "ex")),
            P("grp"),
            P("hid", ("ex", "sub")),
            P("sub", "hid"),
            P("ex", "hid"),
        ),
        out_specs=P("grp", "sub"),
        check_vma=False,
    )
```

```python
import functools
import math

import jax
import jax.numpy as jnp
from jax import lax
from jax.experimental import pallas as pl
from jax.experimental.pallas import tpu as pltpu
from jax.sharding import PartitionSpec as P

D = 4096
FF = 11008
TC_DEV = 128
EX_DEV = 2
QLEN = 16
PAD = 1
MIB = 1024 * 1024
TILE = 256
WIDTHS = (1024, 1024)
F32 = jnp.float32
BF16 = jnp.bfloat16
VMEM = pl.BlockSpec(memory_space=pltpu.VMEM)
SMEM = pl.BlockSpec(memory_space=pltpu.SMEM)
ANY = pl.BlockSpec(memory_space=pl.ANY)
HBM = pl.BlockSpec(memory_space=pltpu.HBM)
ORDER = jax.ShapeDtypeStruct((8, 128), F32)
QUICK = pl.CostEstimate(flops=1024, bytes_accessed=1024, transcendentals=0)


def params(mib):
    return pltpu.CompilerParams(vmem_limit_bytes=mib * MIB)


def chunk_bounds(total):
    bounds = []
    start = 0
    for width in WIDTHS:
        if start + width < total:
            bounds.append((start, width))
            start += width
    bounds.append((start, total - start))
    return bounds


def total_of(values):
    return functools.reduce(lambda a, b: a + b, values)


def column_tiles(width):
    return [(start, min(TILE, width - start)) for start in range(0, width, TILE)]


def basis_copies(basis_hbm, basis_ref, sems, first):
    depth = basis_hbm.shape[0]
    upper = depth // 32 * 16
    copies = []
    for n, (start, size) in enumerate(column_tiles(basis_ref.shape[1])):
        copies.append(
            [
                pltpu.make_async_copy(
                    basis_hbm.at[top : top + rows, first + start : first + start + size],
                    basis_ref.at[top : top + rows, start : start + size],
                    sems.at[n, half],
                )
                for half, (top, rows) in enumerate(((0, upper), (upper, depth - upper)))
            ]
        )
    return copies


def project_kernel(terms, far, first, order_ref, *refs):
    del order_ref
    arrays = refs[: 2 * terms] if terms else ()
    if terms:
        basis_hbm, wide_ref, send_ref, rows_ref, done_ref = refs[2 * terms : 2 * terms + 5]
        scratch = refs[2 * terms + 5 :]
    else:
        rows_ref, basis_hbm, wide_ref, send_ref, done_ref = refs[:5]
        scratch = refs[5:]
    basis_ref, sems = scratch[:2]
    copies = basis_copies(basis_hbm, basis_ref, sems, first)
    if far:
        taken, row_sems = scratch[2:]
        row_copies = [
            pltpu.make_async_copy(a, taken.at[n], row_sems.at[n]) for n, a in enumerate(arrays)
        ]
        for copy in row_copies:
            copy.start()
    for pair in copies:
        for copy in pair:
            copy.start()
    if terms:
        split = arrays[0].shape[1]
        for n in range(2):
            if far:
                row_copies[n].wait()
                rows_ref[n * split : (n + 1) * split] = taken[n].T
            else:
                part = total_of([r[...] for r in arrays[n * terms : (n + 1) * terms]])
                rows_ref[n * split : (n + 1) * split] = part.T
    for pair, (start, size) in zip(copies, column_tiles(basis_ref.shape[1])):
        for copy in pair:
            copy.wait()
        product = jnp.dot(
            rows_ref[...], basis_ref[:, start : start + size], preferred_element_type=F32
        )
        wide_ref[:, start : start + size] = product
        send_ref[:, start : start + size] = product.astype(send_ref.dtype)
    done_ref[...] = jnp.zeros_like(done_ref)


def project(order, inputs, basis, start, width, far=False):
    depth = basis.shape[0]
    tiles = len(column_tiles(width))
    scratch = [pltpu.VMEM((depth, width), basis.dtype), pltpu.SemaphoreType.DMA((tiles, 2))]
    if isinstance(inputs, tuple):
        terms = len(inputs[0])
        arrays = list(inputs[0]) + list(inputs[1])
        rows = 2 * arrays[0].shape[1]
        specs = [HBM if far else VMEM] * (2 * terms)
        if far:
            scratch += [
                pltpu.VMEM((2,) + arrays[0].shape, BF16),
                pltpu.SemaphoreType.DMA((2,)),
            ]
    else:
        terms = 0
        arrays = [inputs]
        rows = inputs.shape[0]
        specs = [VMEM]
    out_shape = [
        jax.ShapeDtypeStruct((rows, width), F32),
        jax.ShapeDtypeStruct((rows, width), BF16),
    ]
    if terms:
        out_shape.append(jax.ShapeDtypeStruct((rows, depth), BF16))
    out = pl.pallas_call(
        functools.partial(project_kernel, terms, far, start),
        in_specs=[ANY] + specs + [HBM],
        out_specs=[VMEM] * (len(out_shape) + 1),
        out_shape=out_shape + [ORDER],
        scratch_shapes=scratch,
        compiler_params=params(59 if far else 48),
        cost_estimate=QUICK,
        name="project",
    )(order, *arrays, basis)
    if terms:
        return out
    return out[0], out[1], inputs, out[2]


def act_kernel(order_ref, cand_ref, query_ref, basis_hbm, share_ref, done_ref, basis_ref, sems):
    del order_ref
    copies = basis_copies(basis_hbm, basis_ref, sems, 0)
    for pair in copies:
        for copy in pair:
            copy.start()
    rows = jnp.concatenate([cand_ref[...], query_ref[...]], 0)
    for pair, (start, size) in zip(copies, column_tiles(basis_ref.shape[1])):
        for copy in pair:
            copy.wait()
        share_ref[:, start : start + size] = jnp.dot(
            rows, basis_ref[:, start : start + size], preferred_element_type=F32
        )
    done_ref[...] = jnp.zeros_like(done_ref)


def act_shares(order, cand_act, query_act, basis):
    rows = cand_act.shape[0] + query_act.shape[0]
    return pl.pallas_call(
        act_kernel,
        in_specs=[ANY, VMEM, VMEM, HBM],
        out_specs=[VMEM, VMEM],
        out_shape=[jax.ShapeDtypeStruct((rows, basis.shape[1]), F32), ORDER],
        scratch_shapes=[
            pltpu.VMEM(basis.shape, basis.dtype),
            pltpu.SemaphoreType.DMA((len(column_tiles(basis.shape[1])), 2)),
        ],
        compiler_params=params(24),
        cost_estimate=QUICK,
        name="acts",
    )(order, cand_act, query_act, basis)


def is_inner():
    spot = lax.axis_index("hid")
    return (spot != 0) & (spot != lax.axis_size("hid") - 1)


def add_kernel(count, order_ref, *refs):
    del order_ref
    sum_ref, done_ref = refs[-2:]
    sum_ref[...] = total_of([r[...].astype(F32) for r in refs[:count]]).astype(sum_ref.dtype)
    done_ref[...] = jnp.zeros_like(done_ref)


def add(order, arrays, after=()):
    return pl.pallas_call(
        functools.partial(add_kernel, len(arrays)),
        in_specs=[ANY] + [VMEM] * len(arrays) + [ANY] * len(after),
        out_specs=[VMEM, VMEM],
        out_shape=[jax.ShapeDtypeStruct(arrays[0].shape, BF16), ORDER],
        compiler_params=params(16),
        cost_estimate=QUICK,
        name="add",
    )(order, *arrays, *after)


def exchange_kernel(order_ref, wide_ref, in_ref, across_ref, next_ref, sum_ref, send_ref, done_ref):
    del order_ref

    @pl.when(is_inner())
    def _():
        total = wide_ref[...] + in_ref[...].astype(F32) + across_ref[...].astype(F32)
        sum_ref[...] = total.astype(BF16)
        send_ref[...] = total.astype(BF16)

    @pl.when(jnp.logical_not(is_inner()))
    def _():
        sum_ref[...] = jnp.zeros_like(sum_ref)
        send_ref[...] = next_ref[...]

    done_ref[...] = jnp.zeros_like(done_ref)


def exchange(order, wide, came_in, across, following):
    shape = jax.ShapeDtypeStruct(wide.shape, BF16)
    return pl.pallas_call(
        exchange_kernel,
        in_specs=[ANY] + [VMEM] * 4,
        out_specs=[VMEM] * 3,
        out_shape=[shape, shape, ORDER],
        compiler_params=params(16),
        cost_estimate=QUICK,
        name="exchange",
    )(order, wide, came_in, across, following)


def masked_kernel(order_ref, share_ref, came_ref, cand_ids_ref, query_ids_ref, acts_ref, done_ref):
    del order_ref
    rows = cand_ids_ref.shape[1]
    for n, ids_ref in enumerate((cand_ids_ref, query_ids_ref)):
        span = slice(n * rows, (n + 1) * rows)
        keep = jnp.where(ids_ref[...] != PAD, 1.0, 0.0).astype(F32)
        keep = jnp.broadcast_to(keep, (rows, rows)).T[:, :1]
        acts_ref[span, :] = ((share_ref[span, :] + came_ref[span, :]) * keep).astype(BF16)
    done_ref[...] = jnp.zeros_like(done_ref)


def masked_acts(order, share, came, cand_ids, query_ids):
    return pl.pallas_call(
        masked_kernel,
        in_specs=[ANY] + [VMEM] * 4,
        out_specs=[VMEM, VMEM],
        out_shape=[jax.ShapeDtypeStruct(share.shape, BF16), ORDER],
        compiler_params=params(16),
        cost_estimate=QUICK,
        name="masked_acts",
    )(order, share, came, cand_ids[None, :], query_ids[None, :])


def split_kernel(examples, order_ref, offsets_ref, own, over, split_ref, query_ref, done_ref):
    del order_ref
    rows, features = own.shape[0] // 2, own.shape[1]
    ex = lax.axis_index("ex")
    spot = lax.broadcasted_iota(jnp.int32, (rows, 1), 0)
    for place, acts in enumerate((own, over)):
        span = slice(place * rows, (place + 1) * rows)
        first = (ex if place == 0 else 1 - ex) * rows
        cand = acts[:rows, :]
        query_ref[span, :] = acts[rows:, :]
        for k in range(examples):
            member = spot + first >= offsets_ref[k]
            if k + 1 < examples:
                member = member & (spot + first < offsets_ref[k + 1])
            member = jnp.where(member, 1.0, 0.0).astype(BF16)
            split_ref[span, k * features : (k + 1) * features] = cand * member
    done_ref[...] = jnp.zeros_like(done_ref)


def split_acts(order, offsets, own, over):
    rows, features = own.shape
    examples = offsets.shape[0]
    return pl.pallas_call(
        functools.partial(split_kernel, examples),
        in_specs=[ANY, SMEM, VMEM, VMEM],
        out_specs=[VMEM] * 3,
        out_shape=[
            jax.ShapeDtypeStruct((rows, examples * features), BF16),
            jax.ShapeDtypeStruct((rows, features), BF16),
            ORDER,
        ],
        compiler_params=params(16),
        cost_estimate=QUICK,
        name="split_acts",
    )(order, offsets, own, over)


def row_tiles(width):
    return [(start, min(512, width - start)) for start in range(0, width, 512)]


def score_kernel(blocks, pick, cand_rows, examples, first, order_ref, *refs):
    del order_ref
    per_block = 2 if pick else 1
    parts = refs[: blocks * per_block]
    eig_hbm, split_ref, query_act_ref, out_ref, done_ref, eig_ref, sems = refs[blocks * per_block :]
    width = parts[0].shape[1]
    base = lax.axis_index("sub") * (eig_hbm.shape[0] // lax.axis_size("sub")) + first
    copies = []
    for n, (start, size) in enumerate(row_tiles(width)):
        pieces = []
        for m, top in enumerate(range(0, size, 128)):
            rows = min(128, size - top)
            pieces.append(
                pltpu.make_async_copy(
                    eig_hbm.at[pl.ds(pl.multiple_of(base + start + top, 8), rows), :],
                    eig_ref.at[pl.ds(start + top, rows), :],
                    sems.at[n, m],
                )
            )
        copies.append(pieces)
    for pieces in copies:
        for copy in pieces:
            copy.start()
    sums = []
    for b in range(blocks):
        here = parts[b * per_block]
        if pick:
            sums.append(jnp.where(is_inner(), here[...], parts[b * per_block + 1][...]))
        else:
            sums.append(here[...])
    features = eig_ref.shape[1]
    cand = jnp.concatenate([s[:cand_rows] for s in sums], 0)
    query = jnp.concatenate([s[cand_rows:] for s in sums], 0)
    scores = [0.0] * examples
    for pieces, (start, size) in zip(copies, row_tiles(width)):
        cand_tile = cand[:, start : start + size].T
        query_tile = query[:, start : start + size].T.astype(F32)
        for copy in pieces:
            copy.wait()
        inverse = 1.0 / eig_ref[start : start + size, :]
        for k in range(examples):
            outer = jnp.dot(
                cand_tile,
                split_ref[:, k * features : (k + 1) * features],
                preferred_element_type=F32,
            )
            weights = (outer * inverse).astype(BF16)
            image = lax.dot_general(
                weights,
                query_act_ref[...],
                (((1,), (1,)), ((), ())),
                preferred_element_type=F32,
            )
            scores[k] = scores[k] + jnp.sum(image * query_tile, axis=0, keepdims=True)
    for k in range(examples):
        out_ref[k : k + 1, :] = scores[k]
    done_ref[...] = jnp.zeros_like(done_ref)


def score_chunk(order, blocks, pick, cand_rows, eigvals, first, split, query_acts, examples):
    parts = [a for block in blocks for a in block]
    width = parts[0].shape[1]
    features = eigvals.shape[1]
    return pl.pallas_call(
        functools.partial(score_kernel, len(blocks), pick, cand_rows, examples, first),
        in_specs=[ANY] + [VMEM] * len(parts) + [HBM, VMEM, VMEM],
        out_specs=[VMEM, VMEM],
        out_shape=[jax.ShapeDtypeStruct((examples, query_acts.shape[0]), F32), ORDER],
        scratch_shapes=[
            pltpu.VMEM((width, features), F32),
            pltpu.SemaphoreType.DMA((len(row_tiles(width)), 4)),
        ],
        compiler_params=params(42),
        cost_estimate=QUICK,
        name="score",
    )(order, *parts, eigvals, split, query_acts)


def small_sum(value, axes):
    size = lax.axis_size(axes)
    if size > 4:
        return lax.psum(value, axes)
    terms = [value]
    for other in range(1, size):
        terms.append(lax.ppermute(value, axes, [(i, i ^ other) for i in range(size)]))
    while len(terms) > 1:
        terms = [a + b for a, b in zip(terms[::2], terms[1::2])]
    return terms[0]


STEPS = (
    "P0 P1 A1 S0 P2 S1 P3 E0 P4 S2 E1 HF P5 S3 E2 S4 F3 SP S5 F4 Z0 F5 Z1 Z2"
)


def token_scores_paired(
    cand_grad, query_grad, cand_act, query_act, cand_ids, query_ids, cand_offsets, basis_g, basis_a, eigvals
):
    rows = cand_grad.shape[0]
    examples = cand_offsets.shape[0]
    bounds = chunk_bounds(basis_g.shape[1])
    count = len(bounds)
    swap = lambda a, axis: lax.ppermute(a, axis, [(0, 1), (1, 0)])
    inward = lambda a: lax.ppermute(a, "hid", [(0, 1), (3, 2)])
    across = lambda a: lax.ppermute(a, "hid", [(1, 2), (2, 1)])
    outward = lambda a: lax.ppermute(a, "hid", [(1, 0), (2, 3)])
    beside = lambda a: lax.ppermute(a, "hid", [(0, 1), (1, 0), (2, 3), (3, 2)])

    tokens = [
        ([cand_grad.T], [query_grad.T]),
        ([swap(cand_grad, "ex").T], [swap(query_grad, "ex").T]),
    ]
    order = jnp.zeros((8, 128), F32)
    wide, sends, ins, crossed, summed, outs = {}, {}, {}, {}, {}, {}
    scores = []
    share = came = acts = acts_over = split = query_acts = None
    for step in STEPS.split():
        kind, c = step[0], int(step[1]) if step[1].isdigit() else None
        if kind == "P":
            block, q = divmod(c, count)
            wide[c], sends[c], tokens[block], order = project(
                order, tokens[block], basis_g, *bounds[q], far=c == 0
            )
            if block == 0:
                ins[c] = inward(sends[c])
        elif step == "A1":
            share, order = act_shares(order, cand_act, query_act, basis_a)
            came = swap(share, "sub")
        elif step == "HF":
            acts, order = masked_acts(order, share, came, cand_ids, query_ids)
            acts_over = swap(acts, "ex")
        elif step == "SP":
            split, query_acts, order = split_acts(order, cand_offsets, acts, acts_over)
        elif kind == "S":
            send, order = add(order, [wide[c], ins[c]])
            crossed[c] = across(send)
        elif kind == "E":
            summed[c], send, order = exchange(
                order, wide[c], ins[c], crossed[c], sends[c + count]
            )
            ins[c + count] = outs[c] = beside(send)
        elif kind == "F":
            summed[c], order = add(order, [wide[c], ins[c], crossed[c]])
            outs[c] = outward(summed[c])
        elif kind == "Z":
            out, order = score_chunk(
                order,
                [(summed[n], outs[n]) for n in (c, count + c)],
                True,
                rows,
                eigvals,
                bounds[c][0],
                split,
                query_acts,
                examples,
            )
            scores.append(out)
    return total_of(scores)


def token_scores_gathered(
    cand_grad, query_grad, cand_act, query_act, cand_ids, query_ids, cand_offsets, basis_g, basis_a, eigvals
):
    gather = lambda a: lax.all_gather(a, "ex", axis=0, tiled=True)
    examples = cand_offsets.shape[0]
    features = basis_a.shape[1]
    order = jnp.zeros((8, 128), F32)
    keep = lambda ids: (ids != PAD).astype(BF16)[:, None]
    share = lambda a: lax.psum(jnp.dot(a, basis_a, preferred_element_type=F32), "sub")
    cands = gather(share(cand_act).astype(BF16) * keep(cand_ids))
    query_acts = gather(share(query_act).astype(BF16) * keep(query_ids))
    cand_rows = cands.shape[0]
    positions = jnp.arange(cand_rows, dtype=jnp.int32)
    example_ends = jnp.concatenate([cand_offsets[1:], jnp.full((1,), cand_rows, jnp.int32)])
    member = (positions[:, None] >= cand_offsets[None, :]) & (
        positions[:, None] < example_ends[None, :]
    )
    split = (member.astype(BF16)[:, :, None] * cands[:, None, :]).reshape(
        cand_rows, examples * features
    )
    tokens = jnp.concatenate([gather(cand_grad), gather(query_grad)], 0)
    scores = []
    for start, width in chunk_bounds(basis_g.shape[1]):
        wide, _, tokens, order = project(order, tokens, basis_g, start, width)
        total = lax.psum(wide, "hid").astype(BF16)
        out, order = score_chunk(
            order, [(total,)], False, cand_rows, eigvals, start, split, query_acts, examples
        )
        scores.append(out)
    return total_of(scores)


def per_device(
    cand_grad,
    query_grad,
    cand_act,
    query_act,
    cand_ids,
    query_ids,
    cand_offsets,
    basis_g,
    basis_a,
    eigvals,
):
    groups = lax.axis_size("ex")
    halves = lax.axis_size("sub")
    ex = lax.axis_index("ex")
    sub = lax.axis_index("sub")
    examples = cand_offsets.shape[0]
    paired = (
        groups == 2
        and halves == 2
        and lax.axis_size("hid") == 4
        and cand_grad.shape[0] == query_grad.shape[0]
    )
    arrays = (
        cand_grad, query_grad, cand_act, query_act, cand_ids, query_ids, cand_offsets, basis_g, basis_a, eigvals
    )
    token_scores = token_scores_paired(*arrays) if paired else token_scores_gathered(*arrays)
    queries = groups * query_grad.shape[0] // QLEN
    partial_value = token_scores.reshape(examples, queries, QLEN).sum(2)
    if paired:
        turned = jnp.roll(partial_value, queries // 2, axis=1)
        partial_value = jnp.where(ex == 0, partial_value, turned)
    total = small_sum(small_sum(partial_value, ("ex", "sub")), "hid")
    mine = lax.dynamic_slice_in_dim(total, sub * (queries // halves), queries // halves, 1)
    factor = 1.0 / math.sqrt(FF * D * QLEN * (TC_DEV // EX_DEV))
    return mine * factor


def solution(mesh):
    return jax.shard_map(
        per_device,
        mesh=mesh,
        in_specs=(
            P(("grp", "ex"), "hid"),
            P(("grp", "ex"), "hid"),
            P(("grp", "ex"), "sub"),
            P(("grp", "ex"), "sub"),
            P(("grp", "ex")),
            P(("grp", "ex")),
            P("grp"),
            P("hid", ("ex", "sub")),
            P("sub", "hid"),
            P("ex", "hid"),
        ),
        out_specs=P("grp", "sub"),
        check_vma=False,
    )
```

```python
import functools
import math

import jax
import jax.numpy as jnp
from jax import lax
from jax.experimental import pallas as pl
from jax.experimental.pallas import tpu as pltpu
from jax.sharding import PartitionSpec as P

D = 4096
FF = 11008
TC_DEV = 128
EX_DEV = 2
QLEN = 16
PAD = 1
MIB = 1024 * 1024
TILE = 512
WIDTHS = (1024, 1024)
F32 = jnp.float32
BF16 = jnp.bfloat16
VMEM = pl.BlockSpec(memory_space=pltpu.VMEM)
SMEM = pl.BlockSpec(memory_space=pltpu.SMEM)
ANY = pl.BlockSpec(memory_space=pl.ANY)
HBM = pl.BlockSpec(memory_space=pltpu.HBM)
ORDER = jax.ShapeDtypeStruct((8, 128), F32)
QUICK = pl.CostEstimate(flops=1024, bytes_accessed=1024, transcendentals=0)


def params(mib):
    return pltpu.CompilerParams(vmem_limit_bytes=mib * MIB)


def chunk_bounds(total):
    bounds = []
    start = 0
    for width in WIDTHS:
        if start + width < total:
            bounds.append((start, width))
            start += width
    bounds.append((start, total - start))
    return bounds


def total_of(values):
    return functools.reduce(lambda a, b: a + b, values)


def column_tiles(width):
    return [(start, min(TILE, width - start)) for start in range(0, width, TILE)]


def basis_copies(basis_hbm, basis_ref, sems, first):
    depth = basis_hbm.shape[0]
    upper = depth // 32 * 16
    copies = []
    for n, (start, size) in enumerate(column_tiles(basis_ref.shape[1])):
        copies.append(
            [
                pltpu.make_async_copy(
                    basis_hbm.at[top : top + rows, first + start : first + start + size],
                    basis_ref.at[top : top + rows, start : start + size],
                    sems.at[n, half],
                )
                for half, (top, rows) in enumerate(((0, upper), (upper, depth - upper)))
            ]
        )
    return copies


def project_kernel(terms, first, order_ref, *refs):
    del order_ref
    arrays = refs[: 2 * terms] if terms else ()
    if terms:
        basis_hbm, wide_ref, send_ref, rows_ref, done_ref = refs[2 * terms : 2 * terms + 5]
        scratch = refs[2 * terms + 5 :]
    else:
        rows_ref, basis_hbm, wide_ref, send_ref, done_ref = refs[:5]
        scratch = refs[5:]
    basis_ref, sems = scratch[:2]
    copies = basis_copies(basis_hbm, basis_ref, sems, first)
    if terms == 1:
        taken, row_sems = scratch[2:]
        row_copies = [
            pltpu.make_async_copy(a, taken.at[n], row_sems.at[n]) for n, a in enumerate(arrays)
        ]
        for copy in row_copies:
            copy.start()
    for pair in copies[: 1 if terms == 1 else None]:
        for copy in pair:
            copy.start()
    if terms:
        split = arrays[0].shape[1]
        for n in range(2):
            if terms == 1:
                row_copies[n].wait()
                rows_ref[n * split : (n + 1) * split] = taken[n].T
            else:
                part = total_of([r[...] for r in arrays[n * terms : (n + 1) * terms]])
                rows_ref[n * split : (n + 1) * split] = part.T
    if terms == 1:
        for pair in copies[1:]:
            for copy in pair:
                copy.start()
    for pair, (start, size) in zip(copies, column_tiles(basis_ref.shape[1])):
        for copy in pair:
            copy.wait()
        product = jnp.dot(
            rows_ref[...], basis_ref[:, start : start + size], preferred_element_type=F32
        )
        wide_ref[:, start : start + size] = product
        send_ref[:, start : start + size] = product.astype(send_ref.dtype)
    done_ref[...] = jnp.zeros_like(done_ref)


def project(order, inputs, basis, start, width):
    depth = basis.shape[0]
    tiles = len(column_tiles(width))
    scratch = [pltpu.VMEM((depth, width), basis.dtype), pltpu.SemaphoreType.DMA((tiles, 2))]
    if isinstance(inputs, tuple):
        terms = len(inputs[0])
        arrays = list(inputs[0]) + list(inputs[1])
        rows = 2 * arrays[0].shape[1]
        specs = [HBM if terms == 1 else VMEM] * (2 * terms)
        if terms == 1:
            scratch += [
                pltpu.VMEM((2,) + arrays[0].shape, BF16),
                pltpu.SemaphoreType.DMA((2,)),
            ]
    else:
        terms = 0
        arrays = [inputs]
        rows = inputs.shape[0]
        specs = [VMEM]
    out_shape = [
        jax.ShapeDtypeStruct((rows, width), F32),
        jax.ShapeDtypeStruct((rows, width), BF16),
    ]
    if terms:
        out_shape.append(jax.ShapeDtypeStruct((rows, depth), BF16))
    out = pl.pallas_call(
        functools.partial(project_kernel, terms, start),
        in_specs=[ANY] + specs + [HBM],
        out_specs=[VMEM] * (len(out_shape) + 1),
        out_shape=out_shape + [ORDER],
        scratch_shapes=scratch,
        compiler_params=params(59 if terms == 1 else 48),
        cost_estimate=QUICK,
        name="project",
    )(order, *arrays, basis)
    if terms:
        return out
    return out[0], out[1], inputs, out[2]


def act_kernel(order_ref, cand_ref, query_ref, basis_hbm, share_ref, done_ref, basis_ref, sems):
    del order_ref
    copies = basis_copies(basis_hbm, basis_ref, sems, 0)
    for pair in copies:
        for copy in pair:
            copy.start()
    rows = jnp.concatenate([cand_ref[...], query_ref[...]], 0)
    for pair, (start, size) in zip(copies, column_tiles(basis_ref.shape[1])):
        for copy in pair:
            copy.wait()
        share_ref[:, start : start + size] = jnp.dot(
            rows, basis_ref[:, start : start + size], preferred_element_type=F32
        )
    done_ref[...] = jnp.zeros_like(done_ref)


def act_shares(order, cand_act, query_act, basis):
    rows = cand_act.shape[0] + query_act.shape[0]
    return pl.pallas_call(
        act_kernel,
        in_specs=[ANY, VMEM, VMEM, HBM],
        out_specs=[VMEM, VMEM],
        out_shape=[jax.ShapeDtypeStruct((rows, basis.shape[1]), F32), ORDER],
        scratch_shapes=[
            pltpu.VMEM(basis.shape, basis.dtype),
            pltpu.SemaphoreType.DMA((len(column_tiles(basis.shape[1])), 2)),
        ],
        compiler_params=params(24),
        cost_estimate=QUICK,
        name="acts",
    )(order, cand_act, query_act, basis)


def is_inner():
    spot = lax.axis_index("hid")
    return (spot != 0) & (spot != lax.axis_size("hid") - 1)


def add_kernel(count, order_ref, *refs):
    del order_ref
    sum_ref, done_ref = refs[-2:]
    sum_ref[...] = total_of([r[...].astype(F32) for r in refs[:count]]).astype(sum_ref.dtype)
    done_ref[...] = jnp.zeros_like(done_ref)


def add(order, arrays, after=()):
    return pl.pallas_call(
        functools.partial(add_kernel, len(arrays)),
        in_specs=[ANY] + [VMEM] * len(arrays) + [ANY] * len(after),
        out_specs=[VMEM, VMEM],
        out_shape=[jax.ShapeDtypeStruct(arrays[0].shape, BF16), ORDER],
        compiler_params=params(16),
        cost_estimate=QUICK,
        name="add",
    )(order, *arrays, *after)


def exchange_kernel(order_ref, wide_ref, in_ref, across_ref, next_ref, sum_ref, send_ref, done_ref):
    del order_ref

    @pl.when(is_inner())
    def _():
        total = wide_ref[...] + in_ref[...].astype(F32) + across_ref[...].astype(F32)
        sum_ref[...] = total.astype(BF16)
        send_ref[...] = total.astype(BF16)

    @pl.when(jnp.logical_not(is_inner()))
    def _():
        sum_ref[...] = jnp.zeros_like(sum_ref)
        send_ref[...] = next_ref[...]

    done_ref[...] = jnp.zeros_like(done_ref)


def exchange(order, wide, came_in, across, following):
    shape = jax.ShapeDtypeStruct(wide.shape, BF16)
    return pl.pallas_call(
        exchange_kernel,
        in_specs=[ANY] + [VMEM] * 4,
        out_specs=[VMEM] * 3,
        out_shape=[shape, shape, ORDER],
        compiler_params=params(16),
        cost_estimate=QUICK,
        name="exchange",
    )(order, wide, came_in, across, following)


def gate_kernel(order_ref, first_ref, second_ref, first_out, second_out, done_ref):
    del order_ref, first_ref, second_ref, first_out, second_out
    done_ref[...] = jnp.zeros_like(done_ref)


def gate(order, first, second):
    shapes = [jax.ShapeDtypeStruct(a.shape, a.dtype) for a in (first, second)]
    return pl.pallas_call(
        gate_kernel,
        in_specs=[ANY] * 3,
        out_specs=[ANY, ANY, VMEM],
        out_shape=shapes + [ORDER],
        input_output_aliases={1: 0, 2: 1},
        compiler_params=params(16),
        cost_estimate=QUICK,
        name="gate",
    )(order, first, second)


def masked_kernel(order_ref, share_ref, came_ref, cand_ids_ref, query_ids_ref, acts_ref, done_ref):
    del order_ref
    rows = cand_ids_ref.shape[1]
    for n, ids_ref in enumerate((cand_ids_ref, query_ids_ref)):
        span = slice(n * rows, (n + 1) * rows)
        keep = jnp.where(ids_ref[...] != PAD, 1.0, 0.0).astype(F32)
        keep = jnp.broadcast_to(keep, (rows, rows)).T[:, :1]
        acts_ref[span, :] = ((share_ref[span, :] + came_ref[span, :]) * keep).astype(BF16)
    done_ref[...] = jnp.zeros_like(done_ref)


def masked_acts(order, share, came, cand_ids, query_ids):
    return pl.pallas_call(
        masked_kernel,
        in_specs=[ANY] + [VMEM] * 4,
        out_specs=[VMEM, VMEM],
        out_shape=[jax.ShapeDtypeStruct(share.shape, BF16), ORDER],
        compiler_params=params(16),
        cost_estimate=QUICK,
        name="masked_acts",
    )(order, share, came, cand_ids[None, :], query_ids[None, :])


def split_kernel(examples, order_ref, offsets_ref, own, over, split_ref, query_ref, done_ref):
    del order_ref
    rows, features = own.shape[0] // 2, own.shape[1]
    ex = lax.axis_index("ex")
    spot = lax.broadcasted_iota(jnp.int32, (rows, 1), 0)
    for place, acts in enumerate((own, over)):
        span = slice(place * rows, (place + 1) * rows)
        first = (ex if place == 0 else 1 - ex) * rows
        cand = acts[:rows, :]
        query_ref[span, :] = acts[rows:, :]
        for k in range(examples):
            member = spot + first >= offsets_ref[k]
            if k + 1 < examples:
                member = member & (spot + first < offsets_ref[k + 1])
            member = jnp.where(member, 1.0, 0.0).astype(BF16)
            split_ref[span, k * features : (k + 1) * features] = cand * member
    done_ref[...] = jnp.zeros_like(done_ref)


def split_acts(order, offsets, own, over):
    rows, features = own.shape
    examples = offsets.shape[0]
    return pl.pallas_call(
        functools.partial(split_kernel, examples),
        in_specs=[ANY, SMEM, VMEM, VMEM],
        out_specs=[VMEM] * 3,
        out_shape=[
            jax.ShapeDtypeStruct((rows, examples * features), BF16),
            jax.ShapeDtypeStruct((rows, features), BF16),
            ORDER,
        ],
        compiler_params=params(16),
        cost_estimate=QUICK,
        name="split_acts",
    )(order, offsets, own, over)


def row_pieces(width):
    return [(start, min(128, width - start)) for start in range(0, width, 128)]


def score_kernel(blocks, pick, cand_rows, examples, first, order_ref, *refs):
    del order_ref
    per_block = 2 if pick else 1
    parts = refs[: blocks * per_block]
    (
        eig_hbm, split_ref, query_act_ref, out_ref, done_ref, eig_ref, weights_ref, sems
    ) = refs[blocks * per_block :]
    width = parts[0].shape[1]
    features = eig_ref.shape[1]
    base = lax.axis_index("sub") * (eig_hbm.shape[0] // lax.axis_size("sub")) + first
    copies = [
        pltpu.make_async_copy(
            eig_hbm.at[pl.ds(pl.multiple_of(base + start, 8), rows), :],
            eig_ref.at[pl.ds(start, rows), :],
            sems.at[n],
        )
        for n, (start, rows) in enumerate(row_pieces(width))
    ]
    for copy in copies:
        copy.start()
    sums = []
    for b in range(blocks):
        here = parts[b * per_block]
        if pick:
            sums.append(jnp.where(is_inner(), here[...], parts[b * per_block + 1][...]))
        else:
            sums.append(here[...])
    cand = jnp.concatenate([s[:cand_rows] for s in sums], 0).T
    query = jnp.concatenate([s[cand_rows:] for s in sums], 0).T.astype(F32)

    def outer_of(k):
        return jnp.dot(
            cand,
            split_ref[:, k * features : (k + 1) * features],
            preferred_element_type=F32,
        )

    outer = outer_of(0)
    for copy in copies:
        copy.wait()
    eig_ref[...] = 1.0 / eig_ref[...]
    for k in range(examples):
        if k > 0:
            outer = outer_of(k)
        weights_ref[k * width : (k + 1) * width, :] = (outer * eig_ref[...]).astype(BF16)
    image = lax.dot_general(
        weights_ref[...],
        query_act_ref[...],
        (((1,), (1,)), ((), ())),
        preferred_element_type=F32,
    )
    for k in range(examples):
        out_ref[k : k + 1, :] = jnp.sum(
            image[k * width : (k + 1) * width] * query, axis=0, keepdims=True
        )
    done_ref[...] = jnp.zeros_like(done_ref)


def score_chunk(order, blocks, pick, cand_rows, eigvals, first, split, query_acts, examples):
    parts = [a for block in blocks for a in block]
    width = parts[0].shape[1]
    features = eigvals.shape[1]
    return pl.pallas_call(
        functools.partial(score_kernel, len(blocks), pick, cand_rows, examples, first),
        in_specs=[ANY] + [VMEM] * len(parts) + [HBM, VMEM, VMEM],
        out_specs=[VMEM, VMEM],
        out_shape=[jax.ShapeDtypeStruct((examples, query_acts.shape[0]), F32), ORDER],
        scratch_shapes=[
            pltpu.VMEM((width, features), F32),
            pltpu.VMEM((examples * width, features), BF16),
            pltpu.SemaphoreType.DMA((len(row_pieces(width)),)),
        ],
        compiler_params=params(42),
        cost_estimate=QUICK,
        name="score",
    )(order, *parts, eigvals, split, query_acts)


def small_sum(value, axes):
    size = lax.axis_size(axes)
    if size > 4:
        return lax.psum(value, axes)
    if axes == "hid":
        for other in (1, 2)[: size // 2]:
            value = value + lax.ppermute(value, axes, [(i, i ^ other) for i in range(size)])
        return value
    terms = [value]
    for other in range(1, size):
        terms.append(lax.ppermute(value, axes, [(i, i ^ other) for i in range(size)]))
    while len(terms) > 1:
        terms = [a + b for a, b in zip(terms[::2], terms[1::2])]
    return terms[0]


STEPS = (
    "P0", "P1", "A1", "XW", "S0", "P2", "S1", "P3", "E0", "P4", "S2", "E1", "HF",
    "P5", "S3", "E2", "S4", "F3", "SP", "S5", "F4", "Z0", "F5", "Z1", "Z2",
)


def token_scores_paired(
    cand_grad, query_grad, cand_act, query_act, cand_ids, query_ids, cand_offsets, basis_g, basis_a, eigvals
):
    rows = cand_grad.shape[0]
    examples = cand_offsets.shape[0]
    both = ("ex", "sub")
    bounds = chunk_bounds(basis_g.shape[1])
    count = len(bounds)
    swap = lambda a, axis: lax.ppermute(a, axis, [(0, 1), (1, 0)])
    inward = lambda a: lax.ppermute(a, "hid", [(0, 1), (3, 2)])
    across = lambda a: lax.ppermute(a, "hid", [(1, 2), (2, 1)])
    outward = lambda a: lax.ppermute(a, "hid", [(1, 0), (2, 3)])
    beside = lambda a: lax.ppermute(a, "hid", [(0, 1), (1, 0), (2, 3), (3, 2)])

    cand_over = lax.ppermute(cand_grad, both, [(0, 2), (2, 0)])
    query_over = lax.ppermute(query_grad, both, [(1, 3), (3, 1)])
    tokens = [([cand_grad.T], [query_grad.T]), None]
    order = jnp.zeros((8, 128), F32)
    wide, sends, ins, crossed, summed, outs = {}, {}, {}, {}, {}, {}
    scores = []
    share = came = acts = acts_over = split = query_acts = None
    for step in STEPS:
        kind, c = step[0], int(step[1]) if step[1].isdigit() else None
        if kind == "P":
            block, q = divmod(c, count)
            wide[c], sends[c], tokens[block], order = project(
                order, tokens[block], basis_g, *bounds[q]
            )
            if block == 0:
                ins[c] = inward(sends[c])
        elif step == "XW":
            cand_turned, query_turned, order = gate(order, cand_over.T, query_over.T)
            cand_across = lax.ppermute(cand_turned, both, [(0, 1), (2, 3)])
            query_across = lax.ppermute(query_turned, both, [(1, 0), (3, 2)])
            tokens[1] = ([cand_turned, cand_across], [query_turned, query_across])
        elif step == "A1":
            share, order = act_shares(order, cand_act, query_act, basis_a)
            came = swap(share, "sub")
        elif step == "HF":
            acts, order = masked_acts(order, share, came, cand_ids, query_ids)
            acts_over = swap(acts, "ex")
        elif step == "SP":
            split, query_acts, order = split_acts(order, cand_offsets, acts, acts_over)
        elif kind == "S":
            send, order = add(order, [wide[c], ins[c]])
            crossed[c] = across(send)
        elif kind == "E":
            summed[c], send, order = exchange(
                order, wide[c], ins[c], crossed[c], sends[c + count]
            )
            ins[c + count] = outs[c] = beside(send)
        elif kind == "F":
            summed[c], order = add(order, [wide[c], ins[c], crossed[c]])
            outs[c] = outward(summed[c])
        elif kind == "Z":
            out, order = score_chunk(
                order,
                [(summed[n], outs[n]) for n in (c, count + c)],
                True,
                rows,
                eigvals,
                bounds[c][0],
                split,
                query_acts,
                examples,
            )
            scores.append(out)
    return total_of(scores)


def token_scores_gathered(
    cand_grad, query_grad, cand_act, query_act, cand_ids, query_ids, cand_offsets, basis_g, basis_a, eigvals
):
    gather = lambda a: lax.all_gather(a, "ex", axis=0, tiled=True)
    examples = cand_offsets.shape[0]
    features = basis_a.shape[1]
    order = jnp.zeros((8, 128), F32)
    keep = lambda ids: (ids != PAD).astype(BF16)[:, None]
    share = lambda a: lax.psum(jnp.dot(a, basis_a, preferred_element_type=F32), "sub")
    cands = gather(share(cand_act).astype(BF16) * keep(cand_ids))
    query_acts = gather(share(query_act).astype(BF16) * keep(query_ids))
    cand_rows = cands.shape[0]
    positions = jnp.arange(cand_rows, dtype=jnp.int32)
    example_ends = jnp.concatenate([cand_offsets[1:], jnp.full((1,), cand_rows, jnp.int32)])
    member = (positions[:, None] >= cand_offsets[None, :]) & (
        positions[:, None] < example_ends[None, :]
    )
    split = (member.astype(BF16)[:, :, None] * cands[:, None, :]).reshape(
        cand_rows, examples * features
    )
    tokens = jnp.concatenate([gather(cand_grad), gather(query_grad)], 0)
    scores = []
    for start, width in chunk_bounds(basis_g.shape[1]):
        wide, _, tokens, order = project(order, tokens, basis_g, start, width)
        total = lax.psum(wide, "hid").astype(BF16)
        out, order = score_chunk(
            order, [(total,)], False, cand_rows, eigvals, start, split, query_acts, examples
        )
        scores.append(out)
    return total_of(scores)


def per_device(
    cand_grad,
    query_grad,
    cand_act,
    query_act,
    cand_ids,
    query_ids,
    cand_offsets,
    basis_g,
    basis_a,
    eigvals,
):
    groups = lax.axis_size("ex")
    halves = lax.axis_size("sub")
    ex = lax.axis_index("ex")
    sub = lax.axis_index("sub")
    examples = cand_offsets.shape[0]
    paired = (
        groups == 2
        and halves == 2
        and lax.axis_size("hid") == 4
        and cand_grad.shape[0] == query_grad.shape[0]
    )
    arrays = (
        cand_grad, query_grad, cand_act, query_act, cand_ids, query_ids, cand_offsets, basis_g, basis_a, eigvals
    )
    token_scores = token_scores_paired(*arrays) if paired else token_scores_gathered(*arrays)
    queries = groups * query_grad.shape[0] // QLEN
    partial_value = token_scores.reshape(examples, queries, QLEN).sum(2)
    if paired:
        turned = jnp.roll(partial_value, queries // 2, axis=1)
        partial_value = jnp.where(ex == 0, partial_value, turned)
    total = small_sum(small_sum(partial_value, ("ex", "sub")), "hid")
    mine = lax.dynamic_slice_in_dim(total, sub * (queries // halves), queries // halves, 1)
    factor = 1.0 / math.sqrt(FF * D * QLEN * (TC_DEV // EX_DEV))
    return mine * factor


def solution(mesh):
    return jax.shard_map(
        per_device,
        mesh=mesh,
        in_specs=(
            P(("grp", "ex"), "hid"),
            P(("grp", "ex"), "hid"),
            P(("grp", "ex"), "sub"),
            P(("grp", "ex"), "sub"),
            P(("grp", "ex")),
            P(("grp", "ex")),
            P("grp"),
            P("hid", ("ex", "sub")),
            P("sub", "hid"),
            P("ex", "hid"),
        ),
        out_specs=P("grp", "sub"),
        check_vma=False,
    )
```

```python
import functools
import math

import jax
import jax.numpy as jnp
from jax import lax
from jax.experimental import pallas as pl
from jax.experimental.pallas import tpu as pltpu
from jax.sharding import PartitionSpec as P

D = 4096
FF = 11008
TC_DEV = 128
EX_DEV = 2
QLEN = 16
PAD = 1
MIB = 1024 * 1024
TILE = 512
WIDTHS = (1024, 1024)
F32 = jnp.float32
BF16 = jnp.bfloat16
VMEM = pl.BlockSpec(memory_space=pltpu.VMEM)
SMEM = pl.BlockSpec(memory_space=pltpu.SMEM)
ANY = pl.BlockSpec(memory_space=pl.ANY)
HBM = pl.BlockSpec(memory_space=pltpu.HBM)
ORDER = jax.ShapeDtypeStruct((8, 128), F32)
QUICK = pl.CostEstimate(flops=1024, bytes_accessed=1024, transcendentals=0)


def params(mib):
    return pltpu.CompilerParams(vmem_limit_bytes=mib * MIB)


def chunk_bounds(total):
    bounds = []
    start = 0
    for width in WIDTHS:
        if start + width < total:
            bounds.append((start, width))
            start += width
    bounds.append((start, total - start))
    return bounds


def total_of(values):
    return functools.reduce(lambda a, b: a + b, values)


def padded(width):
    return -(-width // 128) * 128


def clear_tail(ref, width, value):
    if width < ref.shape[1]:
        ref[:, ref.shape[1] - 128 :] = jnp.full((ref.shape[0], 128), value, ref.dtype)


def column_tiles(width):
    return [(start, min(TILE, width - start)) for start in range(0, width, TILE)]


def basis_copies(basis_hbm, basis_ref, sems, first, width, ragged_ref=None):
    depth = basis_hbm.shape[0]
    upper = depth // 32 * 16
    copies = []
    for n, (start, size) in enumerate(column_tiles(width)):
        copies.append(
            [
                pltpu.make_async_copy(
                    basis_hbm.at[top : top + rows, first + start : first + start + size],
                    (
                        ragged_ref.at[top : top + rows, :]
                        if size % 128
                        else basis_ref.at[top : top + rows, start : start + size]
                    ),
                    sems.at[n, half],
                )
                for half, (top, rows) in enumerate(((0, upper), (upper, depth - upper)))
            ]
        )
    return copies


def project_kernel(terms, first, order_ref, *refs):
    del order_ref
    arrays = refs[: 2 * terms] if terms else ()
    if terms:
        basis_hbm, wide_ref, send_ref, rows_ref, done_ref = refs[2 * terms : 2 * terms + 5]
        scratch = refs[2 * terms + 5 :]
    else:
        rows_ref, basis_hbm, wide_ref, send_ref, done_ref = refs[:5]
        scratch = refs[5:]
    basis_ref, sems = scratch[:2]
    ragged_ref = scratch[-1]
    width = wide_ref.shape[1]
    clear_tail(basis_ref, width, 0)
    copies = basis_copies(basis_hbm, basis_ref, sems, first, width, ragged_ref)
    if terms == 1:
        taken, row_sems = scratch[2:4]
        row_copies = [
            pltpu.make_async_copy(a, taken.at[n], row_sems.at[n]) for n, a in enumerate(arrays)
        ]
        for copy in row_copies:
            copy.start()
    for pair in copies[: 1 if terms == 1 else None]:
        for copy in pair:
            copy.start()
    if terms:
        split = arrays[0].shape[1]
        for n in range(2):
            if terms == 1:
                row_copies[n].wait()
                rows_ref[n * split : (n + 1) * split] = taken[n].T
            else:
                part = total_of([r[...] for r in arrays[n * terms : (n + 1) * terms]])
                rows_ref[n * split : (n + 1) * split] = part.T
    if terms == 1:
        for pair in copies[1:]:
            for copy in pair:
                copy.start()
    for pair, (start, size) in zip(copies, column_tiles(width)):
        for copy in pair:
            copy.wait()
        if size % 128:
            basis_ref[:, start : start + size] = ragged_ref[...]
        product = jnp.dot(
            rows_ref[...],
            basis_ref[:, start : start + padded(size)],
            preferred_element_type=F32,
        )[:, :size]
        wide_ref[:, start : start + size] = product
        send_ref[:, start : start + size] = product.astype(send_ref.dtype)
    done_ref[...] = jnp.zeros_like(done_ref)


def project(order, inputs, basis, start, width):
    depth = basis.shape[0]
    tiles = len(column_tiles(width))
    scratch = [pltpu.VMEM((depth, padded(width)), basis.dtype), pltpu.SemaphoreType.DMA((tiles, 2))]
    if isinstance(inputs, tuple):
        terms = len(inputs[0])
        arrays = list(inputs[0]) + list(inputs[1])
        rows = 2 * arrays[0].shape[1]
        specs = [HBM if terms == 1 else VMEM] * (2 * terms)
        if terms == 1:
            scratch += [
                pltpu.VMEM((2,) + arrays[0].shape, BF16),
                pltpu.SemaphoreType.DMA((2,)),
            ]
    else:
        terms = 0
        arrays = [inputs]
        rows = inputs.shape[0]
        specs = [VMEM]
    ragged = column_tiles(width)[-1][1]
    if ragged % 128:
        scratch.append(pltpu.VMEM((depth, ragged), basis.dtype))
    out_shape = [
        jax.ShapeDtypeStruct((rows, width), F32),
        jax.ShapeDtypeStruct((rows, width), BF16),
    ]
    if terms:
        out_shape.append(jax.ShapeDtypeStruct((rows, depth), BF16))
    out = pl.pallas_call(
        functools.partial(project_kernel, terms, start),
        in_specs=[ANY] + specs + [HBM],
        out_specs=[VMEM] * (len(out_shape) + 1),
        out_shape=out_shape + [ORDER],
        scratch_shapes=scratch,
        compiler_params=params(59 if terms == 1 else 48),
        cost_estimate=QUICK,
        name="project",
    )(order, *arrays, basis)
    if terms:
        return out
    return out[0], out[1], inputs, out[2]


def act_kernel(order_ref, cand_ref, query_ref, basis_hbm, share_ref, done_ref, basis_ref, sems):
    del order_ref
    copies = basis_copies(basis_hbm, basis_ref, sems, 0, share_ref.shape[1])
    for pair in copies:
        for copy in pair:
            copy.start()
    rows = jnp.concatenate([cand_ref[...], query_ref[...]], 0)
    for pair, (start, size) in zip(copies, column_tiles(basis_ref.shape[1])):
        for copy in pair:
            copy.wait()
        share_ref[:, start : start + size] = jnp.dot(
            rows, basis_ref[:, start : start + size], preferred_element_type=F32
        )
    done_ref[...] = jnp.zeros_like(done_ref)


def act_shares(order, cand_act, query_act, basis):
    rows = cand_act.shape[0] + query_act.shape[0]
    return pl.pallas_call(
        act_kernel,
        in_specs=[ANY, VMEM, VMEM, HBM],
        out_specs=[VMEM, VMEM],
        out_shape=[jax.ShapeDtypeStruct((rows, basis.shape[1]), F32), ORDER],
        scratch_shapes=[
            pltpu.VMEM(basis.shape, basis.dtype),
            pltpu.SemaphoreType.DMA((len(column_tiles(basis.shape[1])), 2)),
        ],
        compiler_params=params(24),
        cost_estimate=QUICK,
        name="acts",
    )(order, cand_act, query_act, basis)


def is_inner():
    spot = lax.axis_index("hid")
    return (spot != 0) & (spot != lax.axis_size("hid") - 1)


def add_kernel(count, order_ref, *refs):
    del order_ref
    sum_ref, done_ref = refs[-2:]
    sum_ref[...] = total_of([r[...].astype(F32) for r in refs[:count]]).astype(sum_ref.dtype)
    done_ref[...] = jnp.zeros_like(done_ref)


def add(order, arrays, after=()):
    return pl.pallas_call(
        functools.partial(add_kernel, len(arrays)),
        in_specs=[ANY] + [VMEM] * len(arrays) + [ANY] * len(after),
        out_specs=[VMEM, VMEM],
        out_shape=[jax.ShapeDtypeStruct(arrays[0].shape, BF16), ORDER],
        compiler_params=params(16),
        cost_estimate=QUICK,
        name="add",
    )(order, *arrays, *after)


def exchange_kernel(order_ref, wide_ref, in_ref, across_ref, next_ref, sum_ref, send_ref, done_ref):
    del order_ref

    @pl.when(is_inner())
    def _():
        total = wide_ref[...] + in_ref[...].astype(F32) + across_ref[...].astype(F32)
        sum_ref[...] = total.astype(BF16)
        send_ref[...] = total.astype(BF16)

    @pl.when(jnp.logical_not(is_inner()))
    def _():
        sum_ref[...] = jnp.zeros_like(sum_ref)
        send_ref[...] = next_ref[...]

    done_ref[...] = jnp.zeros_like(done_ref)


def exchange(order, wide, came_in, across, following):
    shape = jax.ShapeDtypeStruct(wide.shape, BF16)
    return pl.pallas_call(
        exchange_kernel,
        in_specs=[ANY] + [VMEM] * 4,
        out_specs=[VMEM] * 3,
        out_shape=[shape, shape, ORDER],
        compiler_params=params(16),
        cost_estimate=QUICK,
        name="exchange",
    )(order, wide, came_in, across, following)


def gate_kernel(order_ref, first_ref, second_ref, first_out, second_out, done_ref):
    del order_ref, first_ref, second_ref, first_out, second_out
    done_ref[...] = jnp.zeros_like(done_ref)


def gate(order, first, second):
    shapes = [jax.ShapeDtypeStruct(a.shape, a.dtype) for a in (first, second)]
    return pl.pallas_call(
        gate_kernel,
        in_specs=[ANY] * 3,
        out_specs=[ANY, ANY, VMEM],
        out_shape=shapes + [ORDER],
        input_output_aliases={1: 0, 2: 1},
        compiler_params=params(16),
        cost_estimate=QUICK,
        name="gate",
    )(order, first, second)


def masked_kernel(order_ref, share_ref, came_ref, cand_ids_ref, query_ids_ref, acts_ref, done_ref):
    del order_ref
    rows = cand_ids_ref.shape[1]
    for n, ids_ref in enumerate((cand_ids_ref, query_ids_ref)):
        span = slice(n * rows, (n + 1) * rows)
        keep = jnp.where(ids_ref[...] != PAD, 1.0, 0.0).astype(F32)
        keep = jnp.broadcast_to(keep, (rows, rows)).T[:, :1]
        acts_ref[span, :] = ((share_ref[span, :] + came_ref[span, :]) * keep).astype(BF16)
    done_ref[...] = jnp.zeros_like(done_ref)


def masked_acts(order, share, came, cand_ids, query_ids):
    return pl.pallas_call(
        masked_kernel,
        in_specs=[ANY] + [VMEM] * 4,
        out_specs=[VMEM, VMEM],
        out_shape=[jax.ShapeDtypeStruct(share.shape, BF16), ORDER],
        compiler_params=params(16),
        cost_estimate=QUICK,
        name="masked_acts",
    )(order, share, came, cand_ids[None, :], query_ids[None, :])


def split_kernel(examples, order_ref, offsets_ref, own, over, split_ref, query_ref, done_ref):
    del order_ref
    rows, features = own.shape[0] // 2, own.shape[1]
    ex = lax.axis_index("ex")
    spot = lax.broadcasted_iota(jnp.int32, (rows, 1), 0)
    for place, acts in enumerate((own, over)):
        span = slice(place * rows, (place + 1) * rows)
        first = (ex if place == 0 else 1 - ex) * rows
        cand = acts[:rows, :]
        query_ref[span, :] = acts[rows:, :]
        for k in range(examples):
            member = spot + first >= offsets_ref[k]
            if k + 1 < examples:
                member = member & (spot + first < offsets_ref[k + 1])
            member = jnp.where(member, 1.0, 0.0).astype(BF16)
            split_ref[span, k * features : (k + 1) * features] = cand * member
    done_ref[...] = jnp.zeros_like(done_ref)


def split_acts(order, offsets, own, over):
    rows, features = own.shape
    examples = offsets.shape[0]
    return pl.pallas_call(
        functools.partial(split_kernel, examples),
        in_specs=[ANY, SMEM, VMEM, VMEM],
        out_specs=[VMEM] * 3,
        out_shape=[
            jax.ShapeDtypeStruct((rows, examples * features), BF16),
            jax.ShapeDtypeStruct((rows, features), BF16),
            ORDER,
        ],
        compiler_params=params(16),
        cost_estimate=QUICK,
        name="split_acts",
    )(order, offsets, own, over)


def row_pieces(width):
    return [(start, min(128, width - start)) for start in range(0, width, 128)]


def score_kernel(blocks, pick, cand_rows, examples, first, order_ref, *refs):
    del order_ref
    per_block = 2 if pick else 1
    parts = refs[: blocks * per_block]
    (
        eig_hbm, split_ref, query_act_ref, out_ref, done_ref, eig_ref, weights_ref, sums_ref, sems
    ) = refs[blocks * per_block :]
    width = parts[0].shape[1]
    features = eig_ref.shape[1]
    base = lax.axis_index("sub") * (eig_hbm.shape[0] // lax.axis_size("sub")) + first
    copies = [
        pltpu.make_async_copy(
            eig_hbm.at[pl.ds(pl.multiple_of(base + start, 8), rows), :],
            eig_ref.at[pl.ds(start, rows), :],
            sems.at[n],
        )
        for n, (start, rows) in enumerate(row_pieces(width))
    ]
    span = eig_ref.shape[0]
    if width < span:
        eig_ref[width:] = jnp.ones((span - width, features), F32)
    for copy in copies:
        copy.start()
    clear_tail(sums_ref, width, 0)
    query_rows = parts[0].shape[0] - cand_rows
    for b in range(blocks):
        total = parts[b * per_block][...]
        if pick:
            total = jnp.where(is_inner(), total, parts[b * per_block + 1][...])
        sums_ref[b * cand_rows : (b + 1) * cand_rows, :width] = total[:cand_rows]
        place = blocks * cand_rows + b * query_rows
        sums_ref[place : place + query_rows, :width] = total[cand_rows:]
    cand = sums_ref[: blocks * cand_rows, :].T
    query = sums_ref[blocks * cand_rows :, :].T.astype(F32)

    def outer_of(k):
        return jnp.dot(
            cand,
            split_ref[:, k * features : (k + 1) * features],
            preferred_element_type=F32,
        )

    outer = outer_of(0)
    for copy in copies:
        copy.wait()
    eig_ref[...] = 1.0 / eig_ref[...]
    for k in range(examples):
        if k > 0:
            outer = outer_of(k)
        weights_ref[k * span : (k + 1) * span, :] = (outer * eig_ref[...]).astype(BF16)
    image = lax.dot_general(
        weights_ref[...],
        query_act_ref[...],
        (((1,), (1,)), ((), ())),
        preferred_element_type=F32,
    )
    for k in range(examples):
        out_ref[k : k + 1, :] = jnp.sum(
            image[k * span : (k + 1) * span] * query, axis=0, keepdims=True
        )
    done_ref[...] = jnp.zeros_like(done_ref)


def score_chunk(order, blocks, pick, cand_rows, eigvals, first, split, query_acts, examples):
    parts = [a for block in blocks for a in block]
    width = parts[0].shape[1]
    features = eigvals.shape[1]
    return pl.pallas_call(
        functools.partial(score_kernel, len(blocks), pick, cand_rows, examples, first),
        in_specs=[ANY] + [VMEM] * len(parts) + [HBM, VMEM, VMEM],
        out_specs=[VMEM, VMEM],
        out_shape=[jax.ShapeDtypeStruct((examples, query_acts.shape[0]), F32), ORDER],
        scratch_shapes=[
            pltpu.VMEM((padded(width), features), F32),
            pltpu.VMEM((examples * padded(width), features), BF16),
            pltpu.VMEM((len(blocks) * parts[0].shape[0], padded(width)), BF16),
            pltpu.SemaphoreType.DMA((len(row_pieces(width)),)),
        ],
        compiler_params=params(36),
        cost_estimate=QUICK,
        name="score",
    )(order, *parts, eigvals, split, query_acts)


def small_sum(value, axes):
    size = lax.axis_size(axes)
    if size > 4:
        return lax.psum(value, axes)
    if axes == "hid":
        for other in (1, 2)[: size // 2]:
            value = value + lax.ppermute(value, axes, [(i, i ^ other) for i in range(size)])
        return value
    terms = [value]
    for other in range(1, size):
        terms.append(lax.ppermute(value, axes, [(i, i ^ other) for i in range(size)]))
    while len(terms) > 1:
        terms = [a + b for a, b in zip(terms[::2], terms[1::2])]
    return terms[0]


STEPS = (
    "P0", "P1", "A1", "XW", "S0", "P2", "S1", "P3", "E0", "P4", "S2", "E1", "HF",
    "P5", "S3", "E2", "S4", "F3", "SP", "S5", "F4", "Z0", "F5", "Z1", "Z2",
)


def token_scores_paired(
    cand_grad, query_grad, cand_act, query_act, cand_ids, query_ids, cand_offsets, basis_g, basis_a, eigvals
):
    rows = cand_grad.shape[0]
    examples = cand_offsets.shape[0]
    both = ("ex", "sub")
    bounds = chunk_bounds(basis_g.shape[1])
    count = len(bounds)
    swap = lambda a, axis: lax.ppermute(a, axis, [(0, 1), (1, 0)])
    inward = lambda a: lax.ppermute(a, "hid", [(0, 1), (3, 2)])
    across = lambda a: lax.ppermute(a, "hid", [(1, 2), (2, 1)])
    outward = lambda a: lax.ppermute(a, "hid", [(1, 0), (2, 3)])
    beside = lambda a: lax.ppermute(a, "hid", [(0, 1), (1, 0), (2, 3), (3, 2)])

    cand_over = lax.ppermute(cand_grad, both, [(0, 2), (2, 0)])
    query_over = lax.ppermute(query_grad, both, [(1, 3), (3, 1)])
    tokens = [([cand_grad.T], [query_grad.T]), None]
    order = jnp.zeros((8, 128), F32)
    wide, sends, ins, crossed, summed, outs = {}, {}, {}, {}, {}, {}
    scores = []
    share = came = acts = acts_over = split = query_acts = None
    for step in STEPS:
        kind, c = step[0], int(step[1]) if step[1].isdigit() else None
        if kind == "P":
            block, q = divmod(c, count)
            wide[c], sends[c], tokens[block], order = project(
                order, tokens[block], basis_g, *bounds[q]
            )
            if block == 0:
                ins[c] = inward(sends[c])
        elif step == "XW":
            cand_turned, query_turned, order = gate(order, cand_over.T, query_over.T)
            cand_across = lax.ppermute(cand_turned, both, [(0, 1), (2, 3)])
            query_across = lax.ppermute(query_turned, both, [(1, 0), (3, 2)])
            tokens[1] = ([cand_turned, cand_across], [query_turned, query_across])
        elif step == "A1":
            share, order = act_shares(order, cand_act, query_act, basis_a)
            came = swap(share, "sub")
        elif step == "HF":
            acts, order = masked_acts(order, share, came, cand_ids, query_ids)
            acts_over = swap(acts, "ex")
        elif step == "SP":
            split, query_acts, order = split_acts(order, cand_offsets, acts, acts_over)
        elif kind == "S":
            send, order = add(order, [wide[c], ins[c]])
            crossed[c] = across(send)
        elif kind == "E":
            summed[c], send, order = exchange(
                order, wide[c], ins[c], crossed[c], sends[c + count]
            )
            ins[c + count] = outs[c] = beside(send)
        elif kind == "F":
            summed[c], order = add(order, [wide[c], ins[c], crossed[c]])
            outs[c] = outward(summed[c])
        elif kind == "Z":
            out, order = score_chunk(
                order,
                [(summed[n], outs[n]) for n in (c, count + c)],
                True,
                rows,
                eigvals,
                bounds[c][0],
                split,
                query_acts,
                examples,
            )
            scores.append(out)
    return total_of(scores)


def token_scores_gathered(
    cand_grad, query_grad, cand_act, query_act, cand_ids, query_ids, cand_offsets, basis_g, basis_a, eigvals
):
    gather = lambda a: lax.all_gather(a, "ex", axis=0, tiled=True)
    examples = cand_offsets.shape[0]
    features = basis_a.shape[1]
    order = jnp.zeros((8, 128), F32)
    keep = lambda ids: (ids != PAD).astype(BF16)[:, None]
    share = lambda a: lax.psum(jnp.dot(a, basis_a, preferred_element_type=F32), "sub")
    cands = gather(share(cand_act).astype(BF16) * keep(cand_ids))
    query_acts = gather(share(query_act).astype(BF16) * keep(query_ids))
    cand_rows = cands.shape[0]
    positions = jnp.arange(cand_rows, dtype=jnp.int32)
    example_ends = jnp.concatenate([cand_offsets[1:], jnp.full((1,), cand_rows, jnp.int32)])
    member = (positions[:, None] >= cand_offsets[None, :]) & (
        positions[:, None] < example_ends[None, :]
    )
    split = (member.astype(BF16)[:, :, None] * cands[:, None, :]).reshape(
        cand_rows, examples * features
    )
    tokens = jnp.concatenate([gather(cand_grad), gather(query_grad)], 0)
    scores = []
    for start, width in chunk_bounds(basis_g.shape[1]):
        wide, _, tokens, order = project(order, tokens, basis_g, start, width)
        total = lax.psum(wide, "hid").astype(BF16)
        out, order = score_chunk(
            order, [(total,)], False, cand_rows, eigvals, start, split, query_acts, examples
        )
        scores.append(out)
    return total_of(scores)


def per_device(
    cand_grad,
    query_grad,
    cand_act,
    query_act,
    cand_ids,
    query_ids,
    cand_offsets,
    basis_g,
    basis_a,
    eigvals,
):
    groups = lax.axis_size("ex")
    halves = lax.axis_size("sub")
    ex = lax.axis_index("ex")
    sub = lax.axis_index("sub")
    examples = cand_offsets.shape[0]
    paired = (
        groups == 2
        and halves == 2
        and lax.axis_size("hid") == 4
        and cand_grad.shape[0] == query_grad.shape[0]
    )
    arrays = (
        cand_grad, query_grad, cand_act, query_act, cand_ids, query_ids, cand_offsets, basis_g, basis_a, eigvals
    )
    token_scores = token_scores_paired(*arrays) if paired else token_scores_gathered(*arrays)
    queries = groups * query_grad.shape[0] // QLEN
    partial_value = token_scores.reshape(examples, queries, QLEN).sum(2)
    if paired:
        turned = jnp.roll(partial_value, queries // 2, axis=1)
        partial_value = jnp.where(ex == 0, partial_value, turned)
    total = small_sum(small_sum(partial_value, ("ex", "sub")), "hid")
    mine = lax.dynamic_slice_in_dim(total, sub * (queries // halves), queries // halves, 1)
    factor = 1.0 / math.sqrt(FF * D * QLEN * (TC_DEV // EX_DEV))
    return mine * factor


def solution(mesh):
    return jax.shard_map(
        per_device,
        mesh=mesh,
        in_specs=(
            P(("grp", "ex"), "hid"),
            P(("grp", "ex"), "hid"),
            P(("grp", "ex"), "sub"),
            P(("grp", "ex"), "sub"),
            P(("grp", "ex")),
            P(("grp", "ex")),
            P("grp"),
            P("hid", ("ex", "sub")),
            P("sub", "hid"),
            P("ex", "hid"),
        ),
        out_specs=P("grp", "sub"),
        check_vma=False,
    )
```
